128 devices in a mesh: seq: 32 (over z_hi, y, x), fsdp: 4 (over z_lo, core).
Axes of the slice: x: 4, y: 4, z: 4 (z_hi: 2, z_lo: 2; z = z_hi * 2 + z_lo), core: 2. Of those that a mesh axis runs over, the one named last changes fastest.
Arguments:
- tokens: float32 [4, 8192, 1024], P('fsdp', 'seq'), may hold values from -6 to 6
- token_pos: int32 [4, 8192], P('fsdp', 'seq'), may hold values from 0 to 8183, as said below
- w_in: bfloat16 [1024, 3072], P('seq', 'fsdp'), may hold values from -0.1875 to 0.1875
- w_mix: bfloat16 [1024, 1024], P('seq', 'fsdp'), may hold values from -0.1875 to 0.1875
- w_gate: bfloat16 [1024, 4608], P('seq', 'fsdp'), may hold values from -0.1875 to 0.1875
- w_up: bfloat16 [1024, 4608], P('seq', 'fsdp'), may hold values from -0.1875 to 0.1875
- w_down: bfloat16 [4608, 1024], P('seq', 'fsdp'), may hold values from -0.1875 to 0.1875
- conv_weight: bfloat16 [3, 1024], P(None, 'fsdp'), may hold values from -3 to 3
- norm_gains: bfloat16 [2, 1024], P(None, 'fsdp'), may hold values from 0.5 to 1.5
- cotangent: float32 [4, 8192, 1024], P('fsdp', 'seq'), may hold values from -6 to 6
Outputs:
- block_out: float32 [4, 8192, 1024], P('fsdp', 'seq')
- grad_tokens: float32 [4, 8192, 1024], P('fsdp', 'seq')
- grad_in: float32 [1024, 3072], P('seq', 'fsdp')
- grad_mix: float32 [1024, 1024], P('seq', 'fsdp')
- grad_gate: float32 [1024, 4608], P('seq', 'fsdp')
- grad_up: float32 [1024, 4608], P('seq', 'fsdp')
- grad_down: float32 [4608, 1024], P('seq', 'fsdp')
- grad_conv: float32 [3, 1024], P(None, 'fsdp')
- grad_gains: float32 [2, 1024], P(None, 'fsdp')
The draws below stay inside these ranges and needn't reach their ends.
Inputs may be any that keep to these rules, and one draw needn't show every extreme that they name: `token_pos`: 0 at the first token of a sequence and one more at each following token of the same sequence within a stream; every stream starts a sequence at its first token.
All inputs are finite; a program needn't handle non-finite values.
Results may differ from the reference program's by a relative error of at most 0.025.
Values may be sent and summed in bfloat16 or wider, within the bound.
No kernel may reach another device: no remote copies, remote signals or barrier semaphores. Data moves between devices by JAX's collectives and lax.ppermute only.
A program may use at most 192 MiB of HBM per device.

```python
import jax
import jax.numpy as jnp
from jax import lax

D = 1024
FF = 4608
KERNEL = 3
STREAMS = 4
LENGTH = 8192
ROWS = 256


def draw_token_pos(key, part):
    edge_total = min(8, ROWS)
    lead_len = jax.random.randint(key, (STREAMS, 1), 1, edge_total)
    trail_len = edge_total - lead_len
    index_row = jnp.arange(LENGTH, dtype=jnp.int32)[None, :]
    tail_start = LENGTH - trail_len
    inner_pos = jnp.where(index_row < tail_start, index_row - lead_len, index_row - tail_start)
    return jnp.where(index_row < lead_len, index_row, inner_pos).astype(jnp.int32)


def levels(key, dims, pieces, low, largest):
    level = 1.0
    for dim, blocks in pieces:
        draws = jax.random.uniform(jax.random.fold_in(jax.random.fold_in(key, 6), dim), (blocks,), jnp.float32, low / len(pieces), largest / len(pieces))
        level = level * jnp.repeat(jnp.exp(draws), dims[dim] // blocks).reshape((-1,) + (1,) * (len(dims) - 1 - dim))
    return level


def normal_values(rng, dims, deviation, bound, cuts=(), held_as=jnp.bfloat16):
    drawn = jax.random.normal(rng, dims, jnp.float32) * deviation
    if len(cuts) > 0:
        drawn = levels(rng, dims, cuts, -0.22, 0.18) * drawn
    return jnp.clip(drawn, min=-bound, max=bound).astype(held_as)


def setup_inputs(seed: int = 0) -> dict:
    seeds = jax.random.split(jax.random.key(seed), 11)
    return {
        "tokens": normal_values(seeds[0], (STREAMS, LENGTH, D), 1.0, 6.0, ((0, 4), (1, 32)), jnp.float32),
        "token_pos": draw_token_pos(jax.random.fold_in(seeds[10], 71), 0),
        "w_in": normal_values(seeds[2], (D, 3 * D), D ** -0.5, 0.1875, ((0, 32), (1, 4))),
        "w_mix": normal_values(seeds[3], (D, D), D ** -0.5, 0.1875, ((0, 32), (1, 4))),
        "w_gate": normal_values(seeds[4], (D, FF), D ** -0.5, 0.1875, ((0, 32), (1, 4))),
        "w_up": normal_values(seeds[5], (D, FF), D ** -0.5, 0.1875, ((0, 32), (1, 4))),
        "w_down": normal_values(seeds[6], (FF, D), (FF // 4) ** -0.5, 0.1875, ((0, 32), (1, 4))),
        "conv_weight": normal_values(seeds[7], (KERNEL, D), 0.6, 3.0, ((1, 4),)),
        "norm_gains": jnp.clip(1.0 + 0.1 * jax.random.normal(seeds[8], (2, D), jnp.float32), 0.5, 1.5).astype(jnp.bfloat16),
        "cotangent": normal_values(seeds[9], (STREAMS, LENGTH, D), 1.0, 6.0, ((0, 4), (1, 32)), jnp.float32),
    }


@jax.custom_vjp
def low(v):
    return lax.optimization_barrier(v.astype(jnp.bfloat16)).astype(jnp.float32)

@jax.custom_vjp
def low_back(v):
    return v

def low_keep(v):
    return (low(v), None)

def low_pass(kept, grad):
    return (grad,)

def back_keep(v):
    return (v, None)

def back_low(kept, grad):
    return (low(grad),)
low.defvjp(low_keep, low_pass)
low_back.defvjp(back_keep, back_low)
EPSILON = 1e-05
top_precision = lax.Precision.HIGHEST

def rms_norm(values, norm_gain):
    normed = values * lax.rsqrt(lax.optimization_barrier(jnp.mean(values * values, axis=-1, keepdims=True)) + EPSILON)
    return normed * norm_gain

def stream(stream_x, token_pos, w_in, w_mix, w_gate, w_up, w_down, conv_taps, gain_rows):
    hidden1 = low(rms_norm(stream_x, gain_rows[0]))
    mixed_in = low_back(jnp.dot(hidden1, w_in, precision=top_precision))
    b_part = mixed_in[:, :D]
    c_part = mixed_in[:, D:2 * D]
    x_part = mixed_in[:, 2 * D:]
    product_bx = low_back(low(b_part * x_part))
    mask_one = (token_pos >= 1).astype(jnp.float32)[:, None]
    mask_two = (token_pos >= 2).astype(jnp.float32)[:, None]
    extended = jnp.concatenate([jnp.zeros((2, D), jnp.float32), product_bx], axis=0)
    conv_val = conv_taps[2] * product_bx + conv_taps[1] * mask_one * extended[1:-1] + conv_taps[0] * mask_two * extended[:-2]
    mixer = low(c_part * conv_val)
    middle = stream_x + low_back(jnp.dot(mixer, w_mix, precision=top_precision))
    hidden2 = low(rms_norm(middle, gain_rows[1]))
    gate_val = low_back(jnp.dot(hidden2, w_gate, precision=top_precision))
    up_val = low_back(jnp.dot(hidden2, w_up, precision=top_precision))
    activation = low(jax.nn.silu(gate_val) * up_val)
    return middle + low_back(jnp.dot(activation, w_down, precision=top_precision))

def reference(tokens, token_pos, w_in, w_mix, w_gate, w_up, w_down, conv_weight, norm_gains, cotangent):

    def whole(tokens, w_in, w_mix, w_gate, w_up, w_down, conv_taps, gain_rows):
        checked = jax.checkpoint(stream)

        def per_stream(stream_pair):
            return checked(stream_pair[0], stream_pair[1], w_in, w_mix, w_gate, w_up, w_down, conv_taps, gain_rows)
        return lax.map(per_stream, (tokens, token_pos))
    block_out, pullback = jax.vjp(whole, tokens, w_in.astype(jnp.float32), w_mix.astype(jnp.float32), w_gate.astype(jnp.float32), w_up.astype(jnp.float32), w_down.astype(jnp.float32), conv_weight.astype(jnp.float32), norm_gains.astype(jnp.float32))
    pulled = pullback(cotangent)
    return (block_out, pulled[0], pulled[1], pulled[2], pulled[3], pulled[4], pulled[5], pulled[6], pulled[7])
```

```python
import jax
import jax.numpy as jnp
from jax import lax
from jax.sharding import Mesh
from jax.sharding import PartitionSpec as P

EPSILON = 1e-05
SEQ = ("zh", "y", "x")
YX = ("y", "x")
FSDP = ("zl", "c")
ALL = SEQ + FSDP
BF16 = jnp.bfloat16
F32 = jnp.float32


def swap(x, axis):
    return lax.ppermute(x, axis, [(0, 1), (1, 0)])


def gather_group(x):
    far = swap(x, "zl")
    near = swap(x, "c")
    far_near = swap(far, "c")
    return jnp.concatenate([x, near, far, far_near], axis=0)


def scatter_group(partial):
    sent = jnp.concatenate([partial[1], partial[3]], axis=0).astype(BF16)
    got = swap(sent, "c").astype(F32)
    rows = partial.shape[1]
    far = swap((partial[2] + got[rows:]).astype(BF16), "zl")
    return partial[0] + got[:rows] + far.astype(F32)


def norm_forward(values, norm_gain):
    inv_rms = lax.rsqrt(jnp.mean(values * values, axis=-1, keepdims=True) + EPSILON)
    normed = values * inv_rms
    return (normed, inv_rms, (normed * norm_gain).astype(BF16))


def norm_backward(grad_hidden, normed, inv_rms, norm_gain):
    grad_normed = grad_hidden * norm_gain
    inner_mean = jnp.mean(grad_normed * normed, axis=-1, keepdims=True)
    return (inv_rms * (grad_normed - normed * inner_mean), jnp.sum(grad_hidden * normed, axis=0))


def dot(a, b, dims):
    return lax.dot_general(a, b, (dims, ((), ())), preferred_element_type=F32)


def pair_device(p, flip):
    q, zh = divmod(p, 2)
    return (zh ^ flip) * 16 + q


IN_ROUTES = [[(f, (3 * f + i) % 4) for f in range(4)] for i in range(3)]
GU_ROUTES = [[(s * 4 + f, pair_device(s, flip) * 4 + f) for s in range(32) for f in range(4)] for flip in (0, 1)]
DOWN_ROUTES = [
    [(s * 4 + f, pair_device(f * 8 + s % 8, flip) * 4 + s // 8) for s in range(32) for f in range(4)] for flip in (0, 1)
]
MIX_ROUTE = [(s * 4 + f, (f * 8 + s % 8) * 4 + s // 8) for s in range(32) for f in range(4)]


def back(route):
    return [(b, a) for a, b in route]


def pair_gather(x, routes):
    mine = lax.ppermute(x, ALL, routes[0])
    other = lax.ppermute(x, ALL, routes[1])
    first = lax.axis_index("zh") == 0
    return jnp.where(first, jnp.stack([mine, other]), jnp.stack([other, mine]))


def pair_scatter(x, routes):
    first = lax.axis_index("zh") == 0
    mine = jnp.where(first, x[0], x[1])
    other = jnp.where(first, x[1], x[0])
    return lax.ppermute(mine, ALL, back(routes[0])).astype(F32) + lax.ppermute(other, ALL, back(routes[1])).astype(F32)


def total_over_seq(x):
    copies = jnp.broadcast_to(x, (32, *x.shape))
    return jnp.sum(lax.all_to_all(copies, SEQ, split_axis=0, concat_axis=0, tiled=True), axis=0)


def local(tokens, token_pos, w_in, w_mix, w_gate, w_up, w_down, conv_weight, norm_gains, cotangent):
    inputs = tokens[0]
    grad_result = cotangent[0]
    rows, model = inputs.shape
    f_index = lax.axis_index(FSDP)
    turn = jnp.where(f_index == 1, 2, jnp.where(f_index == 2, 1, 0))

    got = [lax.ppermute(w_in[:, 256 * i : 256 * (i + 1)], FSDP, IN_ROUTES[i]) for i in range(3)]
    in_blocks = lax.dynamic_slice_in_dim(jnp.stack(got + got[:2]), (3 - turn) % 3, 3, axis=0)
    mix_block = lax.ppermute(w_mix, ALL, MIX_ROUTE)
    first_pack = jnp.concatenate([in_blocks.reshape(96, 256), mix_block], axis=0)
    first_all = lax.all_to_all(jnp.broadcast_to(first_pack, (32, 128, 256)), SEQ, 0, 0, tiled=True).reshape(32, 128, 256)
    w_in_f = jnp.concatenate([first_all[:, 32 * i : 32 * (i + 1)].reshape(1024, 256) for i in range(3)], axis=1)
    w_mix_f = jnp.concatenate([first_all[8 * i : 8 * (i + 1), 96:].reshape(256, 256) for i in range(4)], axis=1)

    gate_up_pair = pair_gather(jnp.concatenate([w_gate, w_up], axis=1), GU_ROUTES)
    down_pair = pair_gather(w_down, DOWN_ROUTES)
    gu_blocks = gate_up_pair.reshape(64, 9, 256).transpose(1, 0, 2).reshape(576, 256)
    second_pack = jnp.concatenate([gu_blocks, down_pair.reshape(288, 256)], axis=0)
    second_all = lax.all_gather(second_pack, YX, axis=0, tiled=True).reshape(16, 864, 256)
    w_gu_f = second_all[:, :576].reshape(16, 9, 64, 256).transpose(0, 2, 1, 3).reshape(1024, 2304)
    w_down_f = second_all[:, 576:].reshape(4, 1152, 256).transpose(1, 0, 2).reshape(1152, 1024)

    gain_rows = lax.all_gather(norm_gains, FSDP, axis=1, tiled=True).astype(F32)
    conv_taps = conv_weight.astype(F32)
    positions = gather_group(jnp.minimum(token_pos, 2).astype(BF16))
    mask_one = (positions >= 1).astype(F32)[:, :, None]
    mask_two = (positions >= 2).astype(F32)[:, :, None]

    normed1, inv_one, hidden1 = norm_forward(inputs, gain_rows[0])
    hidden1_all = gather_group(hidden1)
    grad_low_all = gather_group(grad_result.astype(BF16))

    mixed = dot(hidden1_all, w_in_f, ((1,), (0,))).reshape(4, rows, 768)
    b_part, c_part, x_part = mixed[..., :256], mixed[..., 256:512], mixed[..., 512:]
    product_bx = (b_part * x_part).astype(BF16)
    arrived = lax.ppermute(product_bx[:, -2:], SEQ, [(i, i + 1) for i in range(31)])
    extended = jnp.concatenate([arrived, product_bx], axis=1).astype(F32)
    current, back_one, back_two = extended[:, 2:], extended[:, 1:-1], extended[:, :-2]
    conv_val = conv_taps[2] * current + conv_taps[1] * mask_one * back_one + conv_taps[0] * mask_two * back_two
    mixer = (c_part * conv_val).astype(BF16).reshape(4 * rows, 256)
    branch = scatter_group(dot(mixer, w_mix_f, ((1,), (0,))).reshape(4, rows, model))
    middle = inputs + branch
    normed2, inv_two, hidden2 = norm_forward(middle, gain_rows[1])
    hidden2_all = gather_group(hidden2)
    gate_up_out = dot(hidden2_all, w_gu_f, ((1,), (0,)))
    gate_val, up_val = gate_up_out[:, :1152], gate_up_out[:, 1152:]
    gate_sig = jax.nn.sigmoid(gate_val)
    silu_val = gate_val * gate_sig
    activation = (silu_val * up_val).astype(BF16)
    result = middle + scatter_group(dot(activation, w_down_f, ((1,), (0,))).reshape(4, rows, model))

    grad_down = dot(activation, grad_low_all, ((0,), (0,))).astype(BF16)
    grad_act = dot(grad_low_all, w_down_f, ((1,), (1,)))
    grad_gate_val = grad_act * up_val * (gate_sig * (1.0 + gate_val * (1.0 - gate_sig)))
    grad_up_val = grad_act * silu_val
    grad_pair = jnp.concatenate([grad_gate_val, grad_up_val], axis=1).astype(BF16)
    grad_gu = dot(hidden2_all, grad_pair, ((0,), (0,))).astype(BF16)
    back_pack = jnp.concatenate(
        [
            grad_gu.reshape(16, 64, 9, 256).transpose(0, 2, 1, 3).reshape(16, 576, 256),
            grad_down.reshape(1152, 4, 256).transpose(1, 0, 2).reshape(16, 288, 256),
        ],
        axis=1,
    ).reshape(16 * 864, 256)
    ffn_sums = lax.psum_scatter(back_pack, YX, scatter_dimension=0, tiled=True)
    gu_sums = ffn_sums[:576].reshape(9, 2, 32, 256).transpose(1, 2, 0, 3).reshape(2, 32, 2304)
    grad_gu_own = pair_scatter(gu_sums, GU_ROUTES)
    grad_down_own = pair_scatter(ffn_sums[576:].reshape(2, 144, 256), DOWN_ROUTES)

    grad_hidden2 = scatter_group(dot(grad_pair, w_gu_f, ((1,), (1,))).reshape(4, rows, model))
    grad_norm_two, gain_two = norm_backward(grad_hidden2, normed2, inv_two, gain_rows[1])
    grad_middle = grad_result + grad_norm_two
    grad_branch_all = gather_group(grad_middle.astype(BF16))
    grad_mix = dot(mixer, grad_branch_all, ((0,), (0,))).astype(BF16)
    grad_mixer = dot(grad_branch_all, w_mix_f, ((1,), (1,))).reshape(4, rows, 256)
    grad_c = grad_mixer * conv_val
    grad_cv = grad_mixer * c_part
    lag_one = grad_cv * mask_one
    lag_two = grad_cv * mask_two
    later = lax.ppermute(
        jnp.concatenate([lag_one[:, :1], lag_two[:, :2]], axis=1), SEQ, [(i + 1, i) for i in range(31)]
    )
    ahead_one = jnp.concatenate([lag_one[:, 1:], later[:, :1]], axis=1)
    ahead_two = jnp.concatenate([lag_two[:, 2:], later[:, 1:]], axis=1)
    grad_bx = conv_taps[2] * grad_cv + conv_taps[1] * ahead_one + conv_taps[0] * ahead_two
    conv_grads = jnp.stack(
        [
            jnp.sum(lag_two * back_two, axis=(0, 1)),
            jnp.sum(lag_one * back_one, axis=(0, 1)),
            jnp.sum(grad_cv * current, axis=(0, 1)),
        ]
    )
    grad_bx_low = lax.optimization_barrier(grad_bx.astype(BF16)).astype(F32)
    grad_mixed = (
        jnp.concatenate([grad_bx_low * x_part, grad_c, grad_bx_low * b_part], axis=-1).astype(BF16).reshape(4 * rows, 768)
    )
    grad_in = dot(hidden1_all, grad_mixed, ((0,), (0,))).astype(BF16)
    first_back = jnp.concatenate(
        [grad_in[:, 256 * i : 256 * (i + 1)].reshape(32, 32, 256) for i in range(3)]
        + [jnp.concatenate([grad_mix[:, 256 * i : 256 * (i + 1)].reshape(8, 32, 256) for i in range(4)], axis=0)],
        axis=1,
    )
    first_sums = jnp.sum(
        lax.all_to_all(first_back, SEQ, 0, 0, tiled=True).reshape(32, 128, 256).astype(F32), axis=0
    ).astype(BF16)
    in_sums = first_sums[:96].reshape(3, 32, 256)
    in_turned = lax.dynamic_slice_in_dim(jnp.concatenate([in_sums, in_sums[:2]]), turn, 3, axis=0)
    grad_in_own = jnp.concatenate(
        [lax.ppermute(in_turned[i], FSDP, back(IN_ROUTES[i])) for i in range(3)], axis=1
    ).astype(F32)
    grad_mix_own = lax.ppermute(first_sums[96:], ALL, back(MIX_ROUTE)).astype(F32)

    grad_hidden1 = scatter_group(dot(grad_mixed, w_in_f, ((1,), (1,))).reshape(4, rows, model))
    grad_norm_one, gain_one = norm_backward(grad_hidden1, normed1, inv_one, gain_rows[0])
    grad_inputs = grad_middle + grad_norm_one

    small = jnp.concatenate([conv_grads.reshape(-1), gain_one, gain_two])
    totals = total_over_seq(small)
    conv_total = totals[:768].reshape(3, 256)
    gain_sums = totals[768:].reshape(2, 4, 256).transpose(1, 0, 2)
    gains_total = jnp.sum(lax.all_to_all(gain_sums, FSDP, 0, 0, tiled=True), axis=0)
    return (
        result[None],
        grad_inputs[None],
        grad_in_own,
        grad_mix_own,
        grad_gu_own[:, :1152],
        grad_gu_own[:, 1152:],
        grad_down_own,
        conv_total,
        gains_total,
    )


def solution(mesh):
    fine = Mesh(mesh.devices.reshape(2, 4, 4, 2, 2), ALL)
    tokens, weight, small = P(FSDP, SEQ, None), P(SEQ, FSDP), P(None, FSDP)
    return jax.shard_map(
        local,
        mesh=fine,
        in_specs=(tokens, P(FSDP, SEQ), weight, weight, weight, weight, weight, small, small, tokens),
        out_specs=(tokens, tokens, weight, weight, weight, weight, weight, small, small),
        check_vma=False,
    )
```

```python
import functools

import jax
import jax.numpy as jnp
from jax import lax
from jax.experimental import pallas as pl
from jax.experimental.pallas import tpu as pltpu
from jax.sharding import Mesh
from jax.sharding import PartitionSpec as P

EPSILON = 1e-05
SEQ = ("zh", "y", "x")
YX = ("y", "x")
FSDP = ("zl", "c")
ALL = SEQ + FSDP
BF16 = jnp.bfloat16
F32 = jnp.float32


def swap(x, axis):
    return lax.ppermute(x, axis, [(0, 1), (1, 0)])


def gather_group(x):
    far = swap(x, "zl")
    near = swap(x, "c")
    far_near = swap(far, "c")
    return jnp.concatenate([x, near, far, far_near], axis=0)


def scatter_group(partial):
    return finish_scatter(partial[0::2], partial[1::2].astype(BF16))


def finish_scatter(keep, send):
    got = swap(send, "c").astype(F32)
    far = swap((keep[1] + got[1]).astype(BF16), "zl")
    return keep[0] + got[0] + far.astype(F32)


def norm_forward(values, norm_gain):
    inv_rms = lax.rsqrt(jnp.mean(values * values, axis=-1, keepdims=True) + EPSILON)
    normed = values * inv_rms
    return (normed, inv_rms, (normed * norm_gain).astype(BF16))


def norm_backward(grad_hidden, normed, inv_rms, norm_gain):
    grad_normed = grad_hidden * norm_gain
    inner_mean = jnp.mean(grad_normed * normed, axis=-1, keepdims=True)
    return (inv_rms * (grad_normed - normed * inner_mean), jnp.sum(grad_hidden * normed, axis=0))


def dot(a, b, dims):
    return lax.dot_general(a, b, (dims, ((), ())), preferred_element_type=F32)


ROW_ROUTE = [(s * 4 + f, (f * 8 + s % 8) * 4 + s // 8) for s in range(32) for f in range(4)]
ROW_BACK = [(b, a) for a, b in ROW_ROUTE]


def in_zh_order(mine, other):
    first = lax.axis_index("zh") == 0
    return jnp.where(first, jnp.stack([mine, other]), jnp.stack([other, mine]))


def in_member_order(x):
    x = jnp.where(lax.axis_index("c") == 1, jnp.stack([x[1], x[0], x[3], x[2]]), x)
    return jnp.where(lax.axis_index("zl") == 1, jnp.stack([x[2], x[3], x[0], x[1]]), x)


def ffn_kernel(rows_t, h_ref, gl_ref, wg_ref, wd_ref, out_keep, out_send, gh_keep, gh_send, packed,
               wj, wdj, act_s, gp_s, out_acc, gh_acc, g_s, d_s, sems):
    j = pl.program_id(0)
    for k in range(3):
        for zh in range(2):
            wj[512 * zh : 512 * (zh + 1), 256 * k : 256 * (k + 1)] = wg_ref[:, zh, 32 * k : 32 * (k + 1), :].reshape(512, 256)
    for i in range(8):
        at = 8 * j + i
        for f in range(4):
            wdj[48 * i : 48 * (i + 1), 256 * f : 256 * (f + 1)] = wd_ref[
                f % 2 * 8 + at // 3, f // 2, pl.ds(pl.multiple_of(at % 3 * 48, 16), 48), :
            ]

    @pl.when(j == 0)
    def _():
        out_acc[...] = jnp.zeros_like(out_acc)
        gh_acc[...] = jnp.zeros_like(gh_acc)

    def step(t, _):
        rows = pl.ds(pl.multiple_of(t * rows_t, rows_t), rows_t)
        gu = dot(h_ref[rows, :], wj[...], ((1,), (0,)))
        gate, up = gu[:, :384], gu[:, 384:]
        sig = jax.nn.sigmoid(gate)
        silu = gate * sig
        act = (silu * up).astype(BF16)
        grad_act = dot(gl_ref[rows, :], wdj[...], ((1,), (1,)))
        d_gate = grad_act * up * (sig * (1.0 + gate * (1.0 - sig)))
        d_up = grad_act * silu
        act_s[rows, :] = act
        gp_s[rows, :384] = d_gate.astype(BF16)
        gp_s[rows, 384:] = d_up.astype(BF16)
        out_acc[rows, :] += dot(act, wdj[...], ((1,), (0,)))
        gh_acc[rows, :] += dot(gp_s[rows, :], wj[...], ((1,), (1,)))
        return 0

    lax.fori_loop(0, 1024 // rows_t, step, 0)
    for k in range(3):
        acc = dot(h_ref[...], gp_s[:, 256 * k : 256 * (k + 1)], ((0,), (0,))).astype(BF16)
        for zh in range(2):
            g_s[j, :, zh, 32 * k : 32 * (k + 1), :] = acc[512 * zh : 512 * (zh + 1)].reshape(16, 32, 256)
    for f in range(4):
        acc = dot(act_s[...], gl_ref[:, 256 * f : 256 * (f + 1)], ((0,), (0,))).astype(BF16)
        for i in range(8):
            at = 8 * j + i
            d_s[f % 2 * 8 + at // 3, f // 2, pl.ds(pl.multiple_of(at % 3 * 48, 16), 48), :] = acc[48 * i : 48 * (i + 1)]

    def send(i):
        return pltpu.make_async_copy(g_s.at[i], packed.at[:, :, pl.ds(96 * i, 96), :], sems.at[i])

    for i in range(3):
        @pl.when(j == i)
        def _():
            send(i).start()

    @pl.when(j == 2)
    def _():
        last = pltpu.make_async_copy(d_s, packed.at[:, :, pl.ds(288, 144), :], sems.at[3])
        last.start()
        for i in range(2):
            out_keep[i] = out_acc[512 * i : 512 * i + 256]
            gh_keep[i] = gh_acc[512 * i : 512 * i + 256]
            out_send[i] = out_acc[512 * i + 256 : 512 * (i + 1)].astype(BF16)
            gh_send[i] = gh_acc[512 * i + 256 : 512 * (i + 1)].astype(BF16)
        for i in range(3):
            send(i).wait()
        last.wait()

def ffn(h, gl, pack, rows_t=512):
    whole = lambda shape: pl.BlockSpec(shape, lambda j: (0,) * len(shape))
    once = lambda shape: pl.BlockSpec(shape, lambda j: (0,) * len(shape), pipeline_mode=pl.Buffered(1))
    half = (2, 256, 1024)
    return pl.pallas_call(
        functools.partial(ffn_kernel, rows_t),
        grid=(3,),
        in_specs=[once((1024, 1024)), once((1024, 1024)), pl.BlockSpec((16, 2, 96, 256), lambda j: (0, 0, j, 0)),
                  pl.BlockSpec((16, 2, 144, 256), lambda j: (0, 0, 2, 0), pipeline_mode=pl.Buffered(1))],
        out_specs=[once(half)] * 4 + [pl.BlockSpec(memory_space=pl.ANY)],
        out_shape=[jax.ShapeDtypeStruct(half, F32), jax.ShapeDtypeStruct(half, BF16)] * 2 + [jax.ShapeDtypeStruct((16, 2, 432, 256), BF16)],
        scratch_shapes=[pltpu.VMEM((1024, 768), BF16), pltpu.VMEM((384, 1024), BF16), pltpu.VMEM((1024, 384), BF16), pltpu.VMEM((1024, 768), BF16),
            pltpu.VMEM((1024, 1024), F32), pltpu.VMEM((1024, 1024), F32), pltpu.VMEM((3, 16, 2, 96, 256), BF16), pltpu.VMEM((16, 2, 144, 256), BF16),
            pltpu.SemaphoreType.DMA((4,))],
        compiler_params=pltpu.CompilerParams(vmem_limit_bytes=56 * 1024 * 1024, dimension_semantics=("arbitrary",)),
        cost_estimate=pl.CostEstimate(flops=22 * 10**9, bytes_accessed=30 * 10**6, transcendentals=2 * 10**6),
    )(h, gl, pack, pack)


def local(tokens, token_pos, w_in, w_mix, w_gate, w_up, w_down, conv_weight, norm_gains, cotangent):
    inputs = tokens[0]
    grad_result = cotangent[0]
    rows, model = inputs.shape
    f_index = lax.axis_index(FSDP)

    line = jnp.concatenate([norm_gains[:1], norm_gains[1:], jnp.minimum(token_pos, 2).astype(BF16)], axis=1)
    start = gather_group(jnp.concatenate([w_in, line, jnp.zeros((15, 768), BF16)], axis=0)[None])
    in_blocks = []
    for part in range(3):
        column = 4 * part + f_index
        at = (column // 3 ^ f_index, 0, column % 3 * 256)
        in_blocks.append(lax.dynamic_slice(start, at, (1, 32, 256))[0])
    gain_rows = in_member_order(start[:, 32, :512].astype(F32)).reshape(4, 2, 256).transpose(1, 0, 2).reshape(2, 1024)
    positions = start[:, 32, 512:]
    mask_one = (positions >= 1).astype(F32)[:, :, None]
    mask_two = (positions >= 2).astype(F32)[:, :, None]
    conv_taps = conv_weight.astype(F32)

    row_blocks = lax.ppermute(jnp.concatenate([w_mix, w_down], axis=0), ALL, ROW_ROUTE)
    first_pack = jnp.concatenate([*in_blocks, row_blocks[:32]], axis=0)
    first_all = lax.all_to_all(jnp.broadcast_to(first_pack, (32, 128, 256)), SEQ, 0, 0, tiled=True).reshape(32, 128, 256)
    w_in_f = jnp.concatenate([first_all[:, 32 * i : 32 * (i + 1)].reshape(1024, 256) for i in range(3)], axis=1)
    w_mix_f = jnp.concatenate([first_all[8 * i : 8 * (i + 1), 96:].reshape(256, 256) for i in range(4)], axis=1)

    pieces = []
    for at in range(0, 1152, 384):
        pieces.append(w_gate[:, at : at + 256])
        pieces.append(jnp.concatenate([w_gate[:, at + 256 : at + 384], w_up[:, at : at + 128]], axis=1))
        pieces.append(w_up[:, at + 128 : at + 384])
    second_own = jnp.concatenate([*pieces, row_blocks[32:]], axis=0)
    second_pack = in_zh_order(second_own, swap(second_own, "zh"))
    second_all = lax.all_gather(second_pack.reshape(864, 256), YX, axis=0, tiled=True).reshape(16, 2, 432, 256)

    normed1, inv_one, hidden1 = norm_forward(inputs, gain_rows[0])
    hidden1_all = gather_group(hidden1)
    grad_low_all = gather_group(grad_result.astype(BF16))

    mixed = dot(hidden1_all, w_in_f, ((1,), (0,))).reshape(4, rows, 768)
    b_part, c_part, x_part = mixed[..., :256], mixed[..., 256:512], mixed[..., 512:]
    product_bx = (b_part * x_part).astype(BF16)
    arrived = lax.ppermute(product_bx[:, -2:], SEQ, [(i, i + 1) for i in range(31)])
    extended = jnp.concatenate([arrived, product_bx], axis=1).astype(F32)
    current, back_one, back_two = extended[:, 2:], extended[:, 1:-1], extended[:, :-2]
    conv_val = conv_taps[2] * current + conv_taps[1] * mask_one * back_one + conv_taps[0] * mask_two * back_two
    mixer = (c_part * conv_val).astype(BF16).reshape(4 * rows, 256)
    branch = scatter_group(dot(mixer, w_mix_f, ((1,), (0,))).reshape(4, rows, model))
    middle = inputs + branch
    normed2, inv_two, hidden2 = norm_forward(middle, gain_rows[1])
    hidden2_all = gather_group(hidden2)

    out_keep, out_send, grad_keep, grad_send, back_pack = ffn(hidden2_all, grad_low_all, second_all)
    ffn_sums = lax.psum_scatter(back_pack.reshape(16 * 864, 256), YX, scatter_dimension=0, tiled=True).reshape(2, 432, 256)
    ordered = in_zh_order(ffn_sums[0], ffn_sums[1])
    ffn_own = ordered[0].astype(F32) + swap(ordered[1], "zh").astype(F32)
    grad_down = lax.ppermute(ffn_own[288:].astype(BF16), ALL, ROW_BACK).astype(F32)

    grad_hidden2 = finish_scatter(grad_keep, grad_send)
    grad_norm_two, gain_two = norm_backward(grad_hidden2, normed2, inv_two, gain_rows[1])
    grad_middle = grad_result + grad_norm_two
    grad_branch_all = gather_group(grad_middle.astype(BF16))
    out_got = swap(out_send, "c").astype(F32)
    out_far, _ = lax.optimization_barrier(((out_keep[1] + out_got[1]).astype(BF16), grad_branch_all))
    out_far = swap(out_far, "zl")
    result = middle + out_keep[0] + out_got[0] + out_far.astype(F32)
    grad_mix = dot(mixer, grad_branch_all, ((0,), (0,))).astype(BF16)
    grad_mixer = dot(grad_branch_all, w_mix_f, ((1,), (1,))).reshape(4, rows, 256)
    grad_c = grad_mixer * conv_val
    grad_cv = grad_mixer * c_part
    lag_one = grad_cv * mask_one
    lag_two = grad_cv * mask_two
    later = lax.ppermute(
        jnp.concatenate([lag_one[:, :1], lag_two[:, :2]], axis=1), SEQ, [(i + 1, i) for i in range(31)]
    )
    ahead_one = jnp.concatenate([lag_one[:, 1:], later[:, :1]], axis=1)
    ahead_two = jnp.concatenate([lag_two[:, 2:], later[:, 1:]], axis=1)
    grad_bx = conv_taps[2] * grad_cv + conv_taps[1] * ahead_one + conv_taps[0] * ahead_two
    conv_grads = jnp.stack(
        [
            jnp.sum(lag_two * back_two, axis=(0, 1)),
            jnp.sum(lag_one * back_one, axis=(0, 1)),
            jnp.sum(grad_cv * current, axis=(0, 1)),
        ]
    )
    grad_bx_low = lax.optimization_barrier(grad_bx.astype(BF16)).astype(F32)
    grad_mixed = (
        jnp.concatenate([grad_bx_low * x_part, grad_c, grad_bx_low * b_part], axis=-1).astype(BF16).reshape(4 * rows, 768)
    )
    grad_in = dot(hidden1_all, grad_mixed, ((0,), (0,)))
    gain_one = jnp.sum(grad_in * w_in_f.astype(F32), axis=1) / gain_rows[0]
    small = jnp.concatenate(
        [gain_one.reshape(4, 256), gain_two.reshape(4, 256), conv_grads, jnp.zeros((5, 256), F32)], axis=0
    ).astype(BF16)
    grad_in = grad_in.astype(BF16)
    first_back = jnp.concatenate(
        [grad_in[:, 256 * i : 256 * (i + 1)].reshape(32, 32, 256) for i in range(3)]
        + [jnp.concatenate([grad_mix[:, 256 * i : 256 * (i + 1)].reshape(8, 32, 256) for i in range(4)], axis=0)]
        + [jnp.broadcast_to(small, (32, 16, 256))],
        axis=1,
    )
    first_back, _ = lax.optimization_barrier((first_back, out_far))
    first_got = lax.all_to_all(first_back, SEQ, 0, 0, tiled=True).reshape(32, 144, 256)
    first_got, _ = lax.optimization_barrier((first_got, grad_down))
    first_sums = jnp.sum(first_got.astype(F32), axis=0)
    conv_total = first_sums[136:139]
    group_sums = gather_group(first_sums[None].astype(BF16))
    in_own = []
    for i in range(3):
        column = 3 * f_index + i
        in_own.append(lax.dynamic_slice(group_sums, (column % 4 ^ f_index, column // 4 * 32, 0), (1, 32, 256))[0])
    grad_in_own = jnp.concatenate(in_own, axis=1).astype(F32)
    gain_terms = group_sums[:, 128:136].reshape(4, 2, 4, 256).astype(F32)
    gains_total = jnp.sum(lax.dynamic_index_in_dim(gain_terms, f_index, axis=2, keepdims=False), axis=0)
    grad_mix_own = lax.ppermute(first_sums[96:128].astype(BF16), ALL, ROW_BACK).astype(F32)

    grad_hidden1 = scatter_group(dot(grad_mixed, w_in_f, ((1,), (1,))).reshape(4, rows, model))
    grad_norm_one, _ = norm_backward(grad_hidden1, normed1, inv_one, gain_rows[0])
    grad_inputs = grad_middle + grad_norm_one

    grad_gu = ffn_own[:288].reshape(9, 32, 256)
    grad_gate = [c for i in (0, 3, 6) for c in (grad_gu[i], grad_gu[i + 1, :, :128])]
    grad_up = [c for i in (0, 3, 6) for c in (grad_gu[i + 1, :, 128:], grad_gu[i + 2])]
    return (
        result[None],
        grad_inputs[None],
        grad_in_own,
        grad_mix_own,
        jnp.concatenate(grad_gate, axis=1),
        jnp.concatenate(grad_up, axis=1),
        grad_down,
        conv_total,
        gains_total,
    )


def solution(mesh):
    fine = Mesh(mesh.devices.reshape(2, 4, 4, 2, 2), ALL)
    tokens, weight, small = P(FSDP, SEQ, None), P(SEQ, FSDP), P(None, FSDP)
    return jax.shard_map(
        local,
        mesh=fine,
        in_specs=(tokens, P(FSDP, SEQ), weight, weight, weight, weight, weight, small, small, tokens),
        out_specs=(tokens, tokens, weight, weight, weight, weight, weight, small, small),
        check_vma=False,
    )
```

```python
import functools

import jax
import jax.numpy as jnp
from jax import lax
from jax.experimental import pallas as pl
from jax.experimental.pallas import tpu as pltpu
from jax.sharding import Mesh
from jax.sharding import PartitionSpec as P

EPSILON = 1e-05
SEQ = ("zh", "y", "x")
YX = ("y", "x")
FSDP = ("zl", "c")
ALL = SEQ + FSDP
BF16 = jnp.bfloat16
F32 = jnp.float32


def swap(x, axis):
    return lax.ppermute(x, axis, [(0, 1), (1, 0)])


def group_blocks(x):
    far = swap(x, "zl")
    near = swap(x, "c")
    return (x, near, far, swap(far, "c"))


def gather_group(x):
    across = lax.ppermute(x, FSDP, [(f, 3 - f) for f in range(4)])
    return jnp.concatenate((x, swap(x, "c"), swap(x, "zl"), across), axis=0)


def after(x, *others):
    return lax.optimization_barrier((x, *others))[0]


def scatter_group(partial):
    return finish_scatter(partial[0::2], partial[1::2].astype(BF16))


def finish_scatter(keep, send):
    got = swap(send, "c").astype(F32)
    far = swap((keep[1] + got[1]).astype(BF16), "zl")
    return keep[0] + got[0] + far.astype(F32)


def norm_forward(values, norm_gain):
    inv_rms = lax.rsqrt(jnp.mean(values * values, axis=-1, keepdims=True) + EPSILON)
    normed = values * inv_rms
    return (normed, inv_rms, (normed * norm_gain).astype(BF16))


def norm_backward(grad_hidden, normed, inv_rms, norm_gain):
    grad_normed = grad_hidden * norm_gain
    inner_mean = jnp.mean(grad_normed * normed, axis=-1, keepdims=True)
    return (inv_rms * (grad_normed - normed * inner_mean), jnp.sum(grad_hidden * normed, axis=0))


def dot(a, b, dims):
    return lax.dot_general(a, b, (dims, ((), ())), preferred_element_type=F32)


ROW_ROUTE = [(s * 4 + f, (f * 8 + s % 8) * 4 + s // 8) for s in range(32) for f in range(4)]
ROW_BACK = [(b, a) for a, b in ROW_ROUTE]
ROW_OTHER = [(a, (b + 64) % 128) for a, b in ROW_ROUTE]


def in_zh_order(mine, other):
    first = lax.axis_index("zh") == 0
    return jnp.where(first, jnp.stack([mine, other]), jnp.stack([other, mine]))


def in_member_order(x):
    x = jnp.where(lax.axis_index("c") == 1, jnp.stack([x[1], x[0], x[3], x[2]]), x)
    return jnp.where(lax.axis_index("zl") == 1, jnp.stack([x[2], x[3], x[0], x[1]]), x)


def ffn_kernel(rows_t, *refs):
    h_blocks, gl_blocks = refs[:4], refs[4:8]
    wg_ref, wd_ref, out_keep, out_send, gh_keep, gh_send, packed = refs[8:15]
    h_ref, gl_ref, wj, wdj, act_s, gp_s, out_acc, gh_acc, g_s, d_s, sems = refs[15:]
    j = pl.program_id(0)
    for k in range(3):
        for zh in range(2):
            wj[512 * zh : 512 * (zh + 1), 256 * k : 256 * (k + 1)] = wg_ref[:, zh, 32 * k : 32 * (k + 1), :].reshape(512, 256)
    for i in range(8):
        at = 8 * j + i
        for f in range(4):
            wdj[48 * i : 48 * (i + 1), 256 * f : 256 * (f + 1)] = wd_ref[
                f % 2 * 8 + at // 3, f // 2, pl.ds(pl.multiple_of(at % 3 * 48, 16), 48), :
            ]

    @pl.when(j == 0)
    def _():
        for i in range(4):
            h_ref[256 * i : 256 * (i + 1), :] = h_blocks[i][...]
            gl_ref[256 * i : 256 * (i + 1), :] = gl_blocks[i][...]
        out_acc[...] = jnp.zeros_like(out_acc)
        gh_acc[...] = jnp.zeros_like(gh_acc)

    def step(t, _):
        rows = pl.ds(pl.multiple_of(t * rows_t, rows_t), rows_t)
        gu = dot(h_ref[rows, :], wj[...], ((1,), (0,)))
        gate, up = gu[:, :384], gu[:, 384:]
        sig = jax.nn.sigmoid(gate)
        silu = gate * sig
        act = (silu * up).astype(BF16)
        grad_act = dot(gl_ref[rows, :], wdj[...], ((1,), (1,)))
        d_gate = grad_act * up * (sig * (1.0 + gate * (1.0 - sig)))
        d_up = grad_act * silu
        act_s[rows, :] = act
        gp_s[rows, :384] = d_gate.astype(BF16)
        gp_s[rows, 384:] = d_up.astype(BF16)
        out_acc[rows, :] += dot(act, wdj[...], ((1,), (0,)))
        gh_acc[rows, :] += dot(gp_s[rows, :], wj[...], ((1,), (1,)))
        return 0

    lax.fori_loop(0, 1024 // rows_t, step, 0)
    for k in range(3):
        acc = dot(h_ref[...], gp_s[:, 256 * k : 256 * (k + 1)], ((0,), (0,))).astype(BF16)
        for zh in range(2):
            g_s[j, :, zh, 32 * k : 32 * (k + 1), :] = acc[512 * zh : 512 * (zh + 1)].reshape(16, 32, 256)
    for f in range(4):
        acc = dot(act_s[...], gl_ref[:, 256 * f : 256 * (f + 1)], ((0,), (0,))).astype(BF16)
        for i in range(8):
            at = 8 * j + i
            d_s[f % 2 * 8 + at // 3, f // 2, pl.ds(pl.multiple_of(at % 3 * 48, 16), 48), :] = acc[48 * i : 48 * (i + 1)]

    def send(i):
        return pltpu.make_async_copy(g_s.at[i], packed.at[:, :, pl.ds(96 * i, 96), :], sems.at[i])

    for i in range(3):
        @pl.when(j == i)
        def _():
            send(i).start()

    @pl.when(j == 2)
    def _():
        last = pltpu.make_async_copy(d_s, packed.at[:, :, pl.ds(288, 144), :], sems.at[3])
        last.start()
        for i in range(2):
            out_keep[i] = out_acc[512 * i : 512 * i + 256]
            gh_keep[i] = gh_acc[512 * i : 512 * i + 256]
            out_send[i] = out_acc[512 * i + 256 : 512 * (i + 1)].astype(BF16)
            gh_send[i] = gh_acc[512 * i + 256 : 512 * (i + 1)].astype(BF16)
        for i in range(3):
            send(i).wait()
        last.wait()

def ffn(h, gl, pack, rows_t=512):
    whole = lambda shape: pl.BlockSpec(shape, lambda j: (0,) * len(shape))
    once = lambda shape: pl.BlockSpec(shape, lambda j: (0,) * len(shape), pipeline_mode=pl.Buffered(1))
    half = (2, 256, 1024)
    return pl.pallas_call(
        functools.partial(ffn_kernel, rows_t),
        grid=(3,),
        in_specs=[once((256, 1024))] * 8 + [pl.BlockSpec((16, 2, 96, 256), lambda j: (0, 0, j, 0)),
                  pl.BlockSpec((16, 2, 144, 256), lambda j: (0, 0, 2, 0), pipeline_mode=pl.Buffered(1))],
        out_specs=[once(half)] * 4 + [pl.BlockSpec(memory_space=pl.ANY)],
        out_shape=[jax.ShapeDtypeStruct(half, F32), jax.ShapeDtypeStruct(half, BF16)] * 2 + [jax.ShapeDtypeStruct((16, 2, 432, 256), BF16)],
        scratch_shapes=[pltpu.VMEM((1024, 1024), BF16)] * 2 + [pltpu.VMEM((1024, 768), BF16), pltpu.VMEM((384, 1024), BF16), pltpu.VMEM((1024, 384), BF16), pltpu.VMEM((1024, 768), BF16),
            pltpu.VMEM((1024, 1024), F32), pltpu.VMEM((1024, 1024), F32), pltpu.VMEM((3, 16, 2, 96, 256), BF16), pltpu.VMEM((16, 2, 144, 256), BF16),
            pltpu.SemaphoreType.DMA((4,))],
        compiler_params=pltpu.CompilerParams(vmem_limit_bytes=56 * 1024 * 1024, dimension_semantics=("arbitrary",)),
        cost_estimate=pl.CostEstimate(flops=22 * 10**9, bytes_accessed=30 * 10**6, transcendentals=2 * 10**6),
    )(*h, *gl, pack, pack)


def mix_back_kernel(gm_ref, gmix_ref, mixed_ref, cv_ref, bx_ref, arrived_ref, later_ref, one_ref, two_ref, taps_ref,
                    h_ref, w_ref, gains_ref, gain_two_ref, back_ref, keep_ref, send_ref, grads, small):
    rows = lax.broadcasted_iota(jnp.int32, (256, 256), 0)
    taps = taps_ref[...]
    tap_grads = [jnp.zeros((1, 256), F32) for _ in range(3)]
    gain_one = jnp.zeros((1, 1024), F32)
    for s in range(4):
        grad_mixer = gm_ref[s]
        b_part, c_part, x_part = (mixed_ref[s, :, 256 * i : 256 * (i + 1)] for i in range(3))
        grad_cv = grad_mixer * c_part
        lag_one, lag_two = grad_cv * one_ref[s], grad_cv * two_ref[s]
        later = later_ref[s]
        ahead_one = jnp.where(rows == 255, later[0:1], pltpu.roll(lag_one, 255, 0))
        ahead_two = jnp.where(rows == 255, later[2:3], jnp.where(rows == 254, later[1:2], pltpu.roll(lag_two, 254, 0)))
        current = bx_ref[s].astype(F32)
        before = arrived_ref[s].astype(F32)
        back_one = jnp.where(rows == 0, before[1:2], pltpu.roll(current, 1, 0))
        back_two = jnp.where(rows == 0, before[0:1], jnp.where(rows == 1, before[1:2], pltpu.roll(current, 2, 0)))
        for i, term in enumerate((lag_two * back_two, lag_one * back_one, grad_cv * current)):
            tap_grads[i] += jnp.sum(term, axis=0, keepdims=True)
        grad_bx = taps[2:3] * grad_cv + taps[1:2] * ahead_one + taps[0:1] * ahead_two
        grad_bx = grad_bx.astype(BF16).astype(F32)
        at = slice(256 * s, 256 * (s + 1))
        grads[at, 0:256] = (grad_bx * x_part).astype(BF16)
        grads[at, 256:512] = (grad_mixer * cv_ref[s]).astype(BF16)
        grads[at, 512:768] = (grad_bx * b_part).astype(BF16)
        grad_h = dot(grads[at, :], w_ref[...], ((1,), (1,)))
        gain_one += jnp.sum(grad_h * h_ref[at, :].astype(F32), axis=0, keepdims=True)
        if s % 2 == 0:
            keep_ref[s // 2] = grad_h
        else:
            send_ref[s // 2] = grad_h.astype(BF16)
    gain_one = gain_one / gains_ref[0:1, :]
    small[...] = jnp.zeros_like(small)
    for i in range(4):
        small[i : i + 1] = gain_one[:, 256 * i : 256 * (i + 1)]
        small[4 + i : 5 + i] = gain_two_ref[:, 256 * i : 256 * (i + 1)]
    for i in range(3):
        small[8 + i : 9 + i] = tap_grads[i]
    back_ref[:, 128:144, :] = jnp.broadcast_to(small[...].astype(BF16)[None], (32, 16, 256))
    for i in range(3):
        grad_in = dot(h_ref[...], grads[:, 256 * i : 256 * (i + 1)], ((0,), (0,)))
        back_ref[:, 32 * i : 32 * (i + 1), :] = grad_in.astype(BF16).reshape(32, 32, 256)
    for i in range(4):
        back_ref[8 * i : 8 * (i + 1), 96:128, :] = gmix_ref[:, 256 * i : 256 * (i + 1)].reshape(8, 32, 256)


def mix_back(*args):
    vmem = pl.BlockSpec(memory_space=pltpu.VMEM)
    half = (2, 256, 1024)
    return pl.pallas_call(
        mix_back_kernel,
        in_specs=[vmem] * len(args),
        out_specs=[vmem] * 3,
        out_shape=[jax.ShapeDtypeStruct((32, 144, 256), BF16), jax.ShapeDtypeStruct(half, F32), jax.ShapeDtypeStruct(half, BF16)],
        scratch_shapes=[pltpu.VMEM((1024, 768), BF16), pltpu.VMEM((16, 256), F32)],
        compiler_params=pltpu.CompilerParams(vmem_limit_bytes=40 * 1024 * 1024),
        cost_estimate=pl.CostEstimate(flops=4 * 10**9, bytes_accessed=10**7, transcendentals=0),
    )(*args)


def pack_columns_kernel(gate_ref, up_ref, out_ref):
    for j in range(3):
        at = 384 * j
        out_ref[96 * j : 96 * j + 32, :] = gate_ref[:, at : at + 256]
        out_ref[96 * j + 32 : 96 * j + 64, 0:128] = gate_ref[:, at + 256 : at + 384]
        out_ref[96 * j + 32 : 96 * j + 64, 128:256] = up_ref[:, at : at + 128]
        out_ref[96 * j + 64 : 96 * j + 96, :] = up_ref[:, at + 128 : at + 384]


def pack_columns(w_gate, w_up):
    vmem = pl.BlockSpec(memory_space=pltpu.VMEM)
    return pl.pallas_call(
        pack_columns_kernel,
        in_specs=[vmem] * 2,
        out_specs=vmem,
        out_shape=jax.ShapeDtypeStruct((288, 256), BF16),
        compiler_params=pltpu.CompilerParams(vmem_limit_bytes=4 * 1024 * 1024),
    )(w_gate, w_up)


def local(tokens, token_pos, w_in, w_mix, w_gate, w_up, w_down, conv_weight, norm_gains, cotangent):
    inputs = tokens[0]
    grad_result = cotangent[0]
    rows, model = inputs.shape
    f_index = lax.axis_index(FSDP)
    grad_low_all = group_blocks(grad_result.astype(BF16))

    line = jnp.concatenate([norm_gains[:1], norm_gains[1:], jnp.minimum(token_pos, 2).astype(BF16)], axis=1)
    start = gather_group(jnp.concatenate([w_in, line, jnp.zeros((15, 768), BF16)], axis=0)[None])
    in_blocks = []
    for part in range(3):
        column = 4 * part + f_index
        at = (column // 3 ^ f_index, 0, column % 3 * 256)
        in_blocks.append(lax.dynamic_slice(start, at, (1, 32, 256))[0])
    gain_rows = in_member_order(start[:, 32, :512].astype(F32)).reshape(4, 2, 256).transpose(1, 0, 2).reshape(2, 1024)
    positions = start[:, 32, 512:]
    mask_one = (positions >= 1).astype(F32)[:, :, None]
    mask_two = (positions >= 2).astype(F32)[:, :, None]
    conv_taps = conv_weight.astype(F32)

    gu_own = pack_columns(w_gate, w_up)
    gu_far = swap(gu_own, "zh")
    row_blocks = lax.ppermute(jnp.concatenate([w_mix, w_down], axis=0), ALL, ROW_ROUTE)
    down_far = lax.ppermute(w_down, ALL, ROW_OTHER)
    second_pack = jnp.concatenate([in_zh_order(gu_own, gu_far), in_zh_order(row_blocks[32:], down_far)], axis=1)
    second_all = lax.all_gather(second_pack.reshape(864, 256), YX, axis=0, tiled=True).reshape(16, 2, 432, 256)

    first_pack = jnp.concatenate([*in_blocks, row_blocks[:32]], axis=0)
    first_all = lax.all_to_all(jnp.broadcast_to(first_pack, (32, 128, 256)), SEQ, 0, 0, tiled=True).reshape(32, 128, 256)
    grad_low_all = group_blocks(grad_result.astype(BF16))
    first_all = after(first_all, *grad_low_all)
    w_in_f = jnp.concatenate([first_all[:, 32 * i : 32 * (i + 1)].reshape(1024, 256) for i in range(3)], axis=1)
    w_mix_f = jnp.concatenate([first_all[8 * i : 8 * (i + 1), 96:].reshape(256, 256) for i in range(4)], axis=1)

    normed1, inv_one, hidden1 = norm_forward(inputs, gain_rows[0])
    hidden1_blocks = group_blocks(hidden1)
    hidden1_all = jnp.concatenate(hidden1_blocks, axis=0)

    mixed = dot(hidden1_all, w_in_f, ((1,), (0,))).reshape(4, rows, 768)
    b_part, c_part, x_part = mixed[..., :256], mixed[..., 256:512], mixed[..., 512:]
    product_bx = (b_part * x_part).astype(BF16)
    arrived = lax.ppermute(product_bx[:, -2:], SEQ, [(i, i + 1) for i in range(31)])
    extended = jnp.concatenate([arrived, product_bx], axis=1).astype(F32)
    current, back_one, back_two = extended[:, 2:], extended[:, 1:-1], extended[:, :-2]
    conv_val = conv_taps[2] * current + conv_taps[1] * mask_one * back_one + conv_taps[0] * mask_two * back_two
    mixer = (c_part * conv_val).astype(BF16).reshape(4 * rows, 256)
    branch = scatter_group(dot(mixer, w_mix_f, ((1,), (0,))).reshape(4, rows, model))
    middle = inputs + branch
    normed2, inv_two, hidden2 = norm_forward(middle, gain_rows[1])
    hidden2_all = group_blocks(hidden2)

    out_keep, out_send, grad_keep, grad_send, back_pack = ffn(hidden2_all, grad_low_all, second_all)
    ffn_sums = lax.psum_scatter(back_pack.reshape(16 * 864, 256), YX, scatter_dimension=0, tiled=True).reshape(2, 432, 256)
    ordered = in_zh_order(ffn_sums[0], ffn_sums[1])
    ffn_own = ordered[0].astype(F32) + swap(ordered[1], "zh").astype(F32)
    grad_down = lax.ppermute(ffn_own[288:].astype(BF16), ALL, ROW_BACK).astype(F32)

    grad_hidden2 = finish_scatter(grad_keep, grad_send)
    grad_norm_two, gain_two = norm_backward(grad_hidden2, normed2, inv_two, gain_rows[1])
    grad_middle = grad_result + grad_norm_two
    grad_branch_all = jnp.concatenate(group_blocks(grad_middle.astype(BF16)), axis=0)
    out_got = swap(out_send, "c").astype(F32)
    out_far, _ = lax.optimization_barrier(((out_keep[1] + out_got[1]).astype(BF16), grad_branch_all))
    out_far = swap(out_far, "zl")
    result = middle + out_keep[0] + out_got[0] + out_far.astype(F32)
    grad_mix = dot(mixer, grad_branch_all, ((0,), (0,))).astype(BF16)
    grad_mixer = dot(grad_branch_all, w_mix_f, ((1,), (1,))).reshape(4, rows, 256)
    edge = grad_mixer[:, :2] * c_part[:, :2]
    later = jnp.concatenate([edge[:, :1] * mask_one[:, :1], edge * mask_two[:, :2]], axis=1)
    later = lax.ppermute(later, SEQ, [(i + 1, i) for i in range(31)])
    first_back, keep, send = mix_back(
        grad_mixer,
        grad_mix,
        mixed,
        conv_val,
        product_bx,
        arrived,
        later,
        mask_one,
        mask_two,
        conv_taps,
        hidden1_all,
        w_in_f,
        gain_rows,
        gain_two[None],
    )
    first_got = lax.all_to_all(first_back, SEQ, 0, 0, tiled=True).reshape(32, 144, 256)
    first_got, _ = lax.optimization_barrier((first_got, grad_down))
    first_sums = jnp.sum(first_got.astype(F32), axis=0)
    conv_total = first_sums[136:139]
    group_sums = gather_group(first_sums[None].astype(BF16))
    in_own = []
    for i in range(3):
        column = 3 * f_index + i
        in_own.append(lax.dynamic_slice(group_sums, (column % 4 ^ f_index, column // 4 * 32, 0), (1, 32, 256))[0])
    grad_in_own = jnp.concatenate(in_own, axis=1).astype(F32)
    gain_terms = group_sums[:, 128:136].reshape(4, 2, 4, 256).astype(F32)
    gains_total = jnp.sum(lax.dynamic_index_in_dim(gain_terms, f_index, axis=2, keepdims=False), axis=0)
    grad_mix_own = lax.ppermute(first_sums[96:128].astype(BF16), ALL, ROW_BACK).astype(F32)

    grad_hidden1 = finish_scatter(keep, send)
    grad_norm_one, _ = norm_backward(grad_hidden1, normed1, inv_one, gain_rows[0])
    grad_inputs = grad_middle + grad_norm_one

    grad_gu = ffn_own[:288].reshape(9, 32, 256)
    grad_gate = [c for i in (0, 3, 6) for c in (grad_gu[i], grad_gu[i + 1, :, :128])]
    grad_up = [c for i in (0, 3, 6) for c in (grad_gu[i + 1, :, 128:], grad_gu[i + 2])]
    return (
        result[None],
        grad_inputs[None],
        grad_in_own,
        grad_mix_own,
        jnp.concatenate(grad_gate, axis=1),
        jnp.concatenate(grad_up, axis=1),
        grad_down,
        conv_total,
        gains_total,
    )


def solution(mesh):
    fine = Mesh(mesh.devices.reshape(2, 4, 4, 2, 2), ALL)
    tokens, weight, small = P(FSDP, SEQ, None), P(SEQ, FSDP), P(None, FSDP)
    return jax.shard_map(
        local,
        mesh=fine,
        in_specs=(tokens, P(FSDP, SEQ), weight, weight, weight, weight, weight, small, small, tokens),
        out_specs=(tokens, tokens, weight, weight, weight, weight, weight, small, small),
        check_vma=False,
    )
```

```python
import functools

import jax
import jax.numpy as jnp
from jax import lax
from jax.experimental import pallas as pl
from jax.experimental.pallas import tpu as pltpu
from jax.sharding import Mesh
from jax.sharding import PartitionSpec as P

EPSILON = 1e-05
SEQ = ("zh", "y", "x")
YX = ("y", "x")
FSDP = ("zl", "c")
ALL = SEQ + FSDP
BF16 = jnp.bfloat16
F32 = jnp.float32


def swap(x, axis):
    return lax.ppermute(x, axis, [(0, 1), (1, 0)])


def group_blocks(x):
    far = swap(x, "zl")
    near = swap(x, "c")
    return (x, near, far, swap(far, "c"))


def gather_group(x):
    across = lax.ppermute(x, FSDP, [(f, 3 - f) for f in range(4)])
    return jnp.concatenate((x, swap(x, "c"), swap(x, "zl"), across), axis=0)


def after(x, *others):
    return lax.optimization_barrier((x, *others))[0]


def scatter_group(partial):
    return finish_scatter(partial[0::2], partial[1::2].astype(BF16))


def finish_scatter(keep, send):
    got = swap(send, "c").astype(F32)
    far = swap((keep[1] + got[1]).astype(BF16), "zl")
    return keep[0] + got[0] + far.astype(F32)


def norm_forward(values, norm_gain):
    inv_rms = lax.rsqrt(jnp.mean(values * values, axis=-1, keepdims=True) + EPSILON)
    normed = values * inv_rms
    return (normed, inv_rms, (normed * norm_gain).astype(BF16))


def norm_backward(grad_hidden, normed, inv_rms, norm_gain):
    grad_normed = grad_hidden * norm_gain
    inner_mean = jnp.mean(grad_normed * normed, axis=-1, keepdims=True)
    return (inv_rms * (grad_normed - normed * inner_mean), jnp.sum(grad_hidden * normed, axis=0))


def dot(a, b, dims):
    return lax.dot_general(a, b, (dims, ((), ())), preferred_element_type=F32)


ROW_ROUTE = [(s * 4 + f, (f * 8 + s % 8) * 4 + s // 8) for s in range(32) for f in range(4)]
ROW_BACK = [(b, a) for a, b in ROW_ROUTE]


def in_zh_order(mine, other):
    first = lax.axis_index("zh") == 0
    return jnp.where(first, jnp.stack([mine, other]), jnp.stack([other, mine]))


def in_member_order(x):
    x = jnp.where(lax.axis_index("c") == 1, jnp.stack([x[1], x[0], x[3], x[2]]), x)
    return jnp.where(lax.axis_index("zl") == 1, jnp.stack([x[2], x[3], x[0], x[1]]), x)


def ffn_kernel(rows_t, *refs):
    h_blocks, gl_blocks = refs[:4], refs[4:8]
    wg_ref, wd_ref, out_keep, out_send, gh_keep, gh_send, packed = refs[8:15]
    h_ref, gl_ref, wj, wdj, act_s, gp_s, out_acc, gh_acc, g_s, d_s, sems = refs[15:]
    j = pl.program_id(0)
    for k in range(3):
        for zh in range(2):
            wj[512 * zh : 512 * (zh + 1), 256 * k : 256 * (k + 1)] = wg_ref[:, zh, 32 * k : 32 * (k + 1), :].reshape(512, 256)
    for i in range(8):
        at = 8 * j + i
        for f in range(4):
            wdj[48 * i : 48 * (i + 1), 256 * f : 256 * (f + 1)] = wd_ref[
                f % 2 * 8 + at // 3, f // 2, pl.ds(pl.multiple_of(at % 3 * 48, 16), 48), :
            ]

    @pl.when(j == 0)
    def _():
        for i in range(4):
            h_ref[256 * i : 256 * (i + 1), :] = h_blocks[i][...]
            gl_ref[256 * i : 256 * (i + 1), :] = gl_blocks[i][...]
        out_acc[...] = jnp.zeros_like(out_acc)
        gh_acc[...] = jnp.zeros_like(gh_acc)

    def step(t, _):
        rows = pl.ds(pl.multiple_of(t * rows_t, rows_t), rows_t)
        gu = dot(h_ref[rows, :], wj[...], ((1,), (0,)))
        gate, up = gu[:, :384], gu[:, 384:]
        sig = jax.nn.sigmoid(gate)
        silu = gate * sig
        act = (silu * up).astype(BF16)
        grad_act = dot(gl_ref[rows, :], wdj[...], ((1,), (1,)))
        d_gate = grad_act * up * (sig * (1.0 + gate * (1.0 - sig)))
        d_up = grad_act * silu
        act_s[rows, :] = act
        gp_s[rows, :384] = d_gate.astype(BF16)
        gp_s[rows, 384:] = d_up.astype(BF16)
        out_acc[rows, :] += dot(act, wdj[...], ((1,), (0,)))
        gh_acc[rows, :] += dot(gp_s[rows, :], wj[...], ((1,), (1,)))
        return 0

    lax.fori_loop(0, 1024 // rows_t, step, 0)
    for k in range(3):
        acc = dot(h_ref[...], gp_s[:, 256 * k : 256 * (k + 1)], ((0,), (0,))).astype(BF16)
        for zh in range(2):
            g_s[j, :, zh, 32 * k : 32 * (k + 1), :] = acc[512 * zh : 512 * (zh + 1)].reshape(16, 32, 256)
    for f in range(4):
        acc = dot(act_s[...], gl_ref[:, 256 * f : 256 * (f + 1)], ((0,), (0,))).astype(BF16)
        for i in range(8):
            at = 8 * j + i
            d_s[f % 2 * 8 + at // 3, f // 2, pl.ds(pl.multiple_of(at % 3 * 48, 16), 48), :] = acc[48 * i : 48 * (i + 1)]

    def send(i):
        return pltpu.make_async_copy(g_s.at[i], packed.at[:, :, pl.ds(96 * i, 96), :], sems.at[i])

    for i in range(3):
        @pl.when(j == i)
        def _():
            send(i).start()

    @pl.when(j == 2)
    def _():
        last = pltpu.make_async_copy(d_s, packed.at[:, :, pl.ds(288, 144), :], sems.at[3])
        last.start()
        for i in range(2):
            out_keep[i] = out_acc[512 * i : 512 * i + 256]
            gh_keep[i] = gh_acc[512 * i : 512 * i + 256]
            out_send[i] = out_acc[512 * i + 256 : 512 * (i + 1)].astype(BF16)
            gh_send[i] = gh_acc[512 * i + 256 : 512 * (i + 1)].astype(BF16)
        for i in range(3):
            send(i).wait()
        last.wait()

def ffn(h, gl, pack, rows_t=512):
    whole = lambda shape: pl.BlockSpec(shape, lambda j: (0,) * len(shape))
    once = lambda shape: pl.BlockSpec(shape, lambda j: (0,) * len(shape), pipeline_mode=pl.Buffered(1))
    half = (2, 256, 1024)
    return pl.pallas_call(
        functools.partial(ffn_kernel, rows_t),
        grid=(3,),
        in_specs=[once((256, 1024))] * 8 + [pl.BlockSpec((16, 2, 96, 256), lambda j: (0, 0, j, 0)),
                  pl.BlockSpec((16, 2, 144, 256), lambda j: (0, 0, 2, 0), pipeline_mode=pl.Buffered(1))],
        out_specs=[once(half)] * 4 + [pl.BlockSpec(memory_space=pl.ANY)],
        out_shape=[jax.ShapeDtypeStruct(half, F32), jax.ShapeDtypeStruct(half, BF16)] * 2 + [jax.ShapeDtypeStruct((16, 2, 432, 256), BF16)],
        scratch_shapes=[pltpu.VMEM((1024, 1024), BF16)] * 2 + [pltpu.VMEM((1024, 768), BF16), pltpu.VMEM((384, 1024), BF16), pltpu.VMEM((1024, 384), BF16), pltpu.VMEM((1024, 768), BF16),
            pltpu.VMEM((1024, 1024), F32), pltpu.VMEM((1024, 1024), F32), pltpu.VMEM((3, 16, 2, 96, 256), BF16), pltpu.VMEM((16, 2, 144, 256), BF16),
            pltpu.SemaphoreType.DMA((4,))],
        compiler_params=pltpu.CompilerParams(vmem_limit_bytes=56 * 1024 * 1024, dimension_semantics=("arbitrary",)),
        cost_estimate=pl.CostEstimate(flops=22 * 10**9, bytes_accessed=30 * 10**6, transcendentals=2 * 10**6),
    )(*h, *gl, pack, pack)


def mix_back_kernel(gm_ref, gmix_ref, mixed_ref, cv_ref, bx_ref, arrived_ref, later_ref, one_ref, two_ref, taps_ref,
                    h_ref, w_ref, gains_ref, gain_two_ref, back_ref, keep_ref, send_ref, grads, small):
    rows = lax.broadcasted_iota(jnp.int32, (256, 256), 0)
    taps = taps_ref[...]
    tap_grads = [jnp.zeros((1, 256), F32) for _ in range(3)]
    gain_one = jnp.zeros((1, 1024), F32)
    for s in range(4):
        grad_mixer = gm_ref[s]
        b_part, c_part, x_part = (mixed_ref[s, :, 256 * i : 256 * (i + 1)] for i in range(3))
        grad_cv = grad_mixer * c_part
        lag_one, lag_two = grad_cv * one_ref[s], grad_cv * two_ref[s]
        later = later_ref[s]
        ahead_one = jnp.where(rows == 255, later[0:1], pltpu.roll(lag_one, 255, 0))
        ahead_two = jnp.where(rows == 255, later[2:3], jnp.where(rows == 254, later[1:2], pltpu.roll(lag_two, 254, 0)))
        current = bx_ref[s].astype(F32)
        before = arrived_ref[s].astype(F32)
        back_one = jnp.where(rows == 0, before[1:2], pltpu.roll(current, 1, 0))
        back_two = jnp.where(rows == 0, before[0:1], jnp.where(rows == 1, before[1:2], pltpu.roll(current, 2, 0)))
        for i, term in enumerate((lag_two * back_two, lag_one * back_one, grad_cv * current)):
            tap_grads[i] += jnp.sum(term, axis=0, keepdims=True)
        grad_bx = taps[2:3] * grad_cv + taps[1:2] * ahead_one + taps[0:1] * ahead_two
        grad_bx = grad_bx.astype(BF16).astype(F32)
        at = slice(256 * s, 256 * (s + 1))
        grads[at, 0:256] = (grad_bx * x_part).astype(BF16)
        grads[at, 256:512] = (grad_mixer * cv_ref[s]).astype(BF16)
        grads[at, 512:768] = (grad_bx * b_part).astype(BF16)
        grad_h = dot(grads[at, :], w_ref[...], ((1,), (1,)))
        gain_one += jnp.sum(grad_h * h_ref[at, :].astype(F32), axis=0, keepdims=True)
        if s % 2 == 0:
            keep_ref[s // 2] = grad_h
        else:
            send_ref[s // 2] = grad_h.astype(BF16)
    gain_one = gain_one / gains_ref[0:1, :]
    small[...] = jnp.zeros_like(small)
    for i in range(4):
        small[i : i + 1] = gain_one[:, 256 * i : 256 * (i + 1)]
        small[4 + i : 5 + i] = gain_two_ref[:, 256 * i : 256 * (i + 1)]
    for i in range(3):
        small[8 + i : 9 + i] = tap_grads[i]
    back_ref[:, 128:144, :] = jnp.broadcast_to(small[...].astype(BF16)[None], (32, 16, 256))
    for i in range(3):
        grad_in = dot(h_ref[...], grads[:, 256 * i : 256 * (i + 1)], ((0,), (0,)))
        back_ref[:, 32 * i : 32 * (i + 1), :] = grad_in.astype(BF16).reshape(32, 32, 256)
    for i in range(4):
        back_ref[8 * i : 8 * (i + 1), 96:128, :] = gmix_ref[:, 256 * i : 256 * (i + 1)].reshape(8, 32, 256)


def mix_back(*args):
    vmem = pl.BlockSpec(memory_space=pltpu.VMEM)
    half = (2, 256, 1024)
    return pl.pallas_call(
        mix_back_kernel,
        in_specs=[vmem] * len(args),
        out_specs=[vmem] * 3,
        out_shape=[jax.ShapeDtypeStruct((32, 144, 256), BF16), jax.ShapeDtypeStruct(half, F32), jax.ShapeDtypeStruct(half, BF16)],
        scratch_shapes=[pltpu.VMEM((1024, 768), BF16), pltpu.VMEM((16, 256), F32)],
        compiler_params=pltpu.CompilerParams(vmem_limit_bytes=40 * 1024 * 1024),
        cost_estimate=pl.CostEstimate(flops=4 * 10**9, bytes_accessed=10**7, transcendentals=0),
    )(*args)


def pack_columns_kernel(gate_ref, up_ref, out_ref):
    for j in range(3):
        at = 384 * j
        out_ref[96 * j : 96 * j + 32, :] = gate_ref[:, at : at + 256]
        out_ref[96 * j + 32 : 96 * j + 64, 0:128] = gate_ref[:, at + 256 : at + 384]
        out_ref[96 * j + 32 : 96 * j + 64, 128:256] = up_ref[:, at : at + 128]
        out_ref[96 * j + 64 : 96 * j + 96, :] = up_ref[:, at + 128 : at + 384]


def pack_columns(w_gate, w_up):
    vmem = pl.BlockSpec(memory_space=pltpu.VMEM)
    return pl.pallas_call(
        pack_columns_kernel,
        in_specs=[vmem] * 2,
        out_specs=vmem,
        out_shape=jax.ShapeDtypeStruct((288, 256), BF16),
        compiler_params=pltpu.CompilerParams(vmem_limit_bytes=4 * 1024 * 1024),
    )(w_gate, w_up)


def local(tokens, token_pos, w_in, w_mix, w_gate, w_up, w_down, conv_weight, norm_gains, cotangent):
    inputs = tokens[0]
    grad_result = cotangent[0]
    rows, model = inputs.shape
    f_index = lax.axis_index(FSDP)

    line = jnp.concatenate([norm_gains[:1], norm_gains[1:], jnp.minimum(token_pos, 2).astype(BF16)], axis=1)
    start = gather_group(jnp.concatenate([w_in, line, jnp.zeros((15, 768), BF16)], axis=0)[None])
    in_blocks = []
    for part in range(3):
        column = 4 * part + f_index
        at = (column // 3 ^ f_index, 0, column % 3 * 256)
        in_blocks.append(lax.dynamic_slice(start, at, (1, 32, 256))[0])
    gain_rows = in_member_order(start[:, 32, :512].astype(F32)).reshape(4, 2, 256).transpose(1, 0, 2).reshape(2, 1024)
    positions = start[:, 32, 512:]
    mask_one = (positions >= 1).astype(F32)[:, :, None]
    mask_two = (positions >= 2).astype(F32)[:, :, None]
    conv_taps = conv_weight.astype(F32)

    row_blocks = lax.ppermute(jnp.concatenate([w_mix, w_down], axis=0), ALL, ROW_ROUTE)
    own = jnp.concatenate([pack_columns(w_gate, w_up), row_blocks[32:], *in_blocks, row_blocks[:32]], axis=0)
    both = in_zh_order(own, swap(own, "zh"))
    first_copies = jnp.broadcast_to(both[:, 432:], (16, 2, 128, 256))
    first_all = lax.all_to_all(first_copies, YX, 0, 0, tiled=True)
    second_all = lax.all_gather(both[:, :432].reshape(864, 256), YX, axis=0, tiled=True).reshape(16, 2, 432, 256)
    grad_low_all = group_blocks(grad_result.astype(BF16))
    first_all = after(first_all, *grad_low_all)
    in_rows = first_all.transpose(1, 0, 2, 3)
    w_in_f = jnp.concatenate([in_rows[:, :, 32 * i : 32 * (i + 1)].reshape(1024, 256) for i in range(3)], axis=1)
    w_mix_f = jnp.concatenate(
        [in_rows[i // 2, i % 2 * 8 : i % 2 * 8 + 8, 96:].reshape(256, 256) for i in range(4)], axis=1
    )

    normed1, inv_one, hidden1 = norm_forward(inputs, gain_rows[0])
    hidden1_blocks = group_blocks(hidden1)
    hidden1_all = jnp.concatenate(hidden1_blocks, axis=0)

    mixed = dot(hidden1_all, w_in_f, ((1,), (0,))).reshape(4, rows, 768)
    b_part, c_part, x_part = mixed[..., :256], mixed[..., 256:512], mixed[..., 512:]
    product_bx = (b_part * x_part).astype(BF16)
    arrived = lax.ppermute(product_bx[:, -2:], SEQ, [(i, i + 1) for i in range(31)])
    extended = jnp.concatenate([arrived, product_bx], axis=1).astype(F32)
    current, back_one, back_two = extended[:, 2:], extended[:, 1:-1], extended[:, :-2]
    conv_val = conv_taps[2] * current + conv_taps[1] * mask_one * back_one + conv_taps[0] * mask_two * back_two
    mixer = (c_part * conv_val).astype(BF16).reshape(4 * rows, 256)
    branch = scatter_group(dot(mixer, w_mix_f, ((1,), (0,))).reshape(4, rows, model))
    middle = inputs + branch
    normed2, inv_two, hidden2 = norm_forward(middle, gain_rows[1])
    hidden2_all = group_blocks(hidden2)

    out_keep, out_send, grad_keep, grad_send, back_pack = ffn(hidden2_all, grad_low_all, second_all)
    ffn_sums = lax.psum_scatter(back_pack.reshape(16 * 864, 256), YX, scatter_dimension=0, tiled=True).reshape(2, 432, 256)
    ordered = in_zh_order(ffn_sums[0], ffn_sums[1])
    ffn_own = ordered[0].astype(F32) + swap(ordered[1], "zh").astype(F32)
    grad_down = lax.ppermute(ffn_own[288:].astype(BF16), ALL, ROW_BACK).astype(F32)

    grad_hidden2 = finish_scatter(grad_keep, grad_send)
    grad_norm_two, gain_two = norm_backward(grad_hidden2, normed2, inv_two, gain_rows[1])
    grad_middle = grad_result + grad_norm_two
    grad_branch_all = jnp.concatenate(group_blocks(grad_middle.astype(BF16)), axis=0)
    out_got = swap(out_send, "c").astype(F32)
    out_far, _ = lax.optimization_barrier(((out_keep[1] + out_got[1]).astype(BF16), grad_branch_all))
    out_far = swap(out_far, "zl")
    result = middle + out_keep[0] + out_got[0] + out_far.astype(F32)
    grad_mix = dot(mixer, grad_branch_all, ((0,), (0,))).astype(BF16)
    grad_mixer = dot(grad_branch_all, w_mix_f, ((1,), (1,))).reshape(4, rows, 256)
    edge = grad_mixer[:, :2] * c_part[:, :2]
    later = jnp.concatenate([edge[:, :1] * mask_one[:, :1], edge * mask_two[:, :2]], axis=1)
    later = lax.ppermute(later, SEQ, [(i + 1, i) for i in range(31)])
    first_back, keep, send = mix_back(
        after(grad_mixer, out_far),
        grad_mix,
        mixed,
        conv_val,
        product_bx,
        arrived,
        later,
        mask_one,
        mask_two,
        conv_taps,
        hidden1_all,
        w_in_f,
        gain_rows,
        gain_two[None],
    )
    first_got = lax.all_to_all(first_back, SEQ, 0, 0, tiled=True).reshape(32, 144, 256)
    first_got, _ = lax.optimization_barrier((first_got, grad_down))
    first_sums = jnp.sum(first_got.astype(F32), axis=0)
    conv_total = first_sums[136:139]
    group_sums = gather_group(first_sums[None].astype(BF16))
    in_own = []
    for i in range(3):
        column = 3 * f_index + i
        in_own.append(lax.dynamic_slice(group_sums, (column % 4 ^ f_index, column // 4 * 32, 0), (1, 32, 256))[0])
    grad_in_own = jnp.concatenate(in_own, axis=1).astype(F32)
    gain_terms = group_sums[:, 128:136].reshape(4, 2, 4, 256).astype(F32)
    gains_total = jnp.sum(lax.dynamic_index_in_dim(gain_terms, f_index, axis=2, keepdims=False), axis=0)
    grad_mix_own = lax.ppermute(first_sums[96:128].astype(BF16), ALL, ROW_BACK).astype(F32)

    grad_hidden1 = finish_scatter(keep, send)
    grad_norm_one, _ = norm_backward(grad_hidden1, normed1, inv_one, gain_rows[0])
    grad_inputs = grad_middle + grad_norm_one

    grad_gu = ffn_own[:288].reshape(9, 32, 256)
    grad_gate = [c for i in (0, 3, 6) for c in (grad_gu[i], grad_gu[i + 1, :, :128])]
    grad_up = [c for i in (0, 3, 6) for c in (grad_gu[i + 1, :, 128:], grad_gu[i + 2])]
    return (
        result[None],
        grad_inputs[None],
        grad_in_own,
        grad_mix_own,
        jnp.concatenate(grad_gate, axis=1),
        jnp.concatenate(grad_up, axis=1),
        grad_down,
        conv_total,
        gains_total,
    )


def solution(mesh):
    fine = Mesh(mesh.devices.reshape(2, 4, 4, 2, 2), ALL)
    tokens, weight, small = P(FSDP, SEQ, None), P(SEQ, FSDP), P(None, FSDP)
    return jax.shard_map(
        local,
        mesh=fine,
        in_specs=(tokens, P(FSDP, SEQ), weight, weight, weight, weight, weight, small, small, tokens),
        out_specs=(tokens, tokens, weight, weight, weight, weight, weight, small, small),
        check_vma=False,
    )
```

```python
import functools

import jax
import jax.numpy as jnp
from jax import lax
from jax.experimental import pallas as pl
from jax.experimental.pallas import tpu as pltpu
from jax.sharding import Mesh
from jax.sharding import PartitionSpec as P

EPSILON = 1e-05
SEQ = ("zh", "y", "x")
YX = ("y", "x")
FSDP = ("zl", "c")
ALL = SEQ + FSDP
BF16 = jnp.bfloat16
F32 = jnp.float32


def swap(x, axis):
    return lax.ppermute(x, axis, [(0, 1), (1, 0)])


def group_blocks(x):
    far = swap(x, "zl")
    near = swap(x, "c")
    return (x, near, far, swap(far, "c"))


def gather_group(x):
    across = lax.ppermute(x, FSDP, [(f, 3 - f) for f in range(4)])
    return jnp.concatenate((x, swap(x, "c"), swap(x, "zl"), across), axis=0)


def after(x, *others):
    return lax.optimization_barrier((x, *others))[0]


def scatter_group(partial):
    return finish_scatter(partial[0::2], partial[1::2].astype(BF16))


def finish_scatter(keep, send):
    got = swap(send, "c").astype(F32)
    far = swap((keep[1] + got[1]).astype(BF16), "zl")
    return keep[0] + got[0] + far.astype(F32)


def norm_forward(values, norm_gain):
    inv_rms = lax.rsqrt(jnp.mean(values * values, axis=-1, keepdims=True) + EPSILON)
    normed = values * inv_rms
    return (normed, inv_rms, (normed * norm_gain).astype(BF16))


def norm_backward(grad_hidden, normed, inv_rms, norm_gain):
    grad_normed = grad_hidden * norm_gain
    inner_mean = jnp.mean(grad_normed * normed, axis=-1, keepdims=True)
    return (inv_rms * (grad_normed - normed * inner_mean), jnp.sum(grad_hidden * normed, axis=0))


def dot(a, b, dims):
    return lax.dot_general(a, b, (dims, ((), ())), preferred_element_type=F32)


ROW_ROUTE = [(s * 4 + f, (f * 8 + s % 8) * 4 + s // 8) for s in range(32) for f in range(4)]
ROW_BACK = [(b, a) for a, b in ROW_ROUTE]


def in_zh_order(mine, other):
    first = lax.axis_index("zh") == 0
    return jnp.where(first, jnp.stack([mine, other]), jnp.stack([other, mine]))


def in_member_order(x):
    x = jnp.where(lax.axis_index("c") == 1, jnp.stack([x[1], x[0], x[3], x[2]]), x)
    return jnp.where(lax.axis_index("zl") == 1, jnp.stack([x[2], x[3], x[0], x[1]]), x)


def ffn_kernel(rows_t, *refs):
    h_blocks, gl_blocks = refs[:4], refs[4:8]
    wg_ref, wd_ref, out_keep, out_send, gh_keep, gh_send, packed = refs[8:15]
    h_ref, gl_ref, wj, wdj, act_s, gp_s, out_acc, gh_acc, g_s, d_s, sems = refs[15:]
    j = pl.program_id(0)
    for k in range(3):
        for zh in range(2):
            wj[512 * zh : 512 * (zh + 1), 256 * k : 256 * (k + 1)] = wg_ref[:, zh, 32 * k : 32 * (k + 1), :].reshape(512, 256)
    for i in range(8):
        at = 8 * j + i
        for f in range(4):
            wdj[48 * i : 48 * (i + 1), 256 * f : 256 * (f + 1)] = wd_ref[
                f % 2 * 8 + at // 3, f // 2, pl.ds(pl.multiple_of(at % 3 * 48, 16), 48), :
            ]

    @pl.when(j == 0)
    def _():
        for i in range(4):
            h_ref[256 * i : 256 * (i + 1), :] = h_blocks[i][...]
            gl_ref[256 * i : 256 * (i + 1), :] = gl_blocks[i][...]
        out_acc[...] = jnp.zeros_like(out_acc)
        gh_acc[...] = jnp.zeros_like(gh_acc)

    def step(t, _):
        rows = pl.ds(pl.multiple_of(t * rows_t, rows_t), rows_t)
        gu = dot(h_ref[rows, :], wj[...], ((1,), (0,)))
        gate, up = gu[:, :384], gu[:, 384:]
        sig = jax.nn.sigmoid(gate)
        silu = gate * sig
        act = (silu * up).astype(BF16)
        grad_act = dot(gl_ref[rows, :], wdj[...], ((1,), (1,)))
        d_gate = grad_act * up * (sig * (1.0 + gate * (1.0 - sig)))
        d_up = grad_act * silu
        act_s[rows, :] = act
        gp_s[rows, :384] = d_gate.astype(BF16)
        gp_s[rows, 384:] = d_up.astype(BF16)
        out_acc[rows, :] += dot(act, wdj[...], ((1,), (0,)))
        gh_acc[rows, :] += dot(gp_s[rows, :], wj[...], ((1,), (1,)))
        return 0

    lax.fori_loop(0, 1024 // rows_t, step, 0)
    for k in range(3):
        acc = dot(h_ref[...], gp_s[:, 256 * k : 256 * (k + 1)], ((0,), (0,))).astype(BF16)
        for zh in range(2):
            g_s[j, :, zh, 32 * k : 32 * (k + 1), :] = acc[512 * zh : 512 * (zh + 1)].reshape(16, 32, 256)
    for f in range(4):
        acc = dot(act_s[...], gl_ref[:, 256 * f : 256 * (f + 1)], ((0,), (0,))).astype(BF16)
        for i in range(8):
            at = 8 * j + i
            d_s[f % 2 * 8 + at // 3, f // 2, pl.ds(pl.multiple_of(at % 3 * 48, 16), 48), :] = acc[48 * i : 48 * (i + 1)]

    def send(i):
        return pltpu.make_async_copy(g_s.at[i], packed.at[:, :, pl.ds(96 * i, 96), :], sems.at[i])

    for i in range(3):
        @pl.when(j == i)
        def _():
            send(i).start()

    @pl.when(j == 2)
    def _():
        last = pltpu.make_async_copy(d_s, packed.at[:, :, pl.ds(288, 144), :], sems.at[3])
        last.start()
        for i in range(2):
            out_keep[i] = out_acc[512 * i : 512 * i + 256]
            gh_keep[i] = gh_acc[512 * i : 512 * i + 256]
            out_send[i] = out_acc[512 * i + 256 : 512 * (i + 1)].astype(BF16)
            gh_send[i] = gh_acc[512 * i + 256 : 512 * (i + 1)].astype(BF16)
        for i in range(3):
            send(i).wait()
        last.wait()

def ffn(h, gl, pack, rows_t=512):
    whole = lambda shape: pl.BlockSpec(shape, lambda j: (0,) * len(shape))
    once = lambda shape: pl.BlockSpec(shape, lambda j: (0,) * len(shape), pipeline_mode=pl.Buffered(1))
    half = (2, 256, 1024)
    return pl.pallas_call(
        functools.partial(ffn_kernel, rows_t),
        grid=(3,),
        in_specs=[once((256, 1024))] * 8 + [pl.BlockSpec((16, 2, 96, 256), lambda j: (0, 0, j, 0)),
                  pl.BlockSpec((16, 2, 144, 256), lambda j: (0, 0, 2, 0), pipeline_mode=pl.Buffered(1))],
        out_specs=[once(half)] * 4 + [pl.BlockSpec(memory_space=pl.ANY)],
        out_shape=[jax.ShapeDtypeStruct(half, F32), jax.ShapeDtypeStruct(half, BF16)] * 2 + [jax.ShapeDtypeStruct((16, 2, 432, 256), BF16)],
        scratch_shapes=[pltpu.VMEM((1024, 1024), BF16)] * 2 + [pltpu.VMEM((1024, 768), BF16), pltpu.VMEM((384, 1024), BF16), pltpu.VMEM((1024, 384), BF16), pltpu.VMEM((1024, 768), BF16),
            pltpu.VMEM((1024, 1024), F32), pltpu.VMEM((1024, 1024), F32), pltpu.VMEM((3, 16, 2, 96, 256), BF16), pltpu.VMEM((16, 2, 144, 256), BF16),
            pltpu.SemaphoreType.DMA((4,))],
        compiler_params=pltpu.CompilerParams(vmem_limit_bytes=56 * 1024 * 1024, dimension_semantics=("arbitrary",)),
        cost_estimate=pl.CostEstimate(flops=22 * 10**9, bytes_accessed=30 * 10**6, transcendentals=2 * 10**6),
    )(*h, *gl, pack, pack)


def mix_back_kernel(gm_ref, gmix_ref, mixed_ref, cv_ref, bx_ref, arrived_ref, later_ref, one_ref, two_ref, taps_ref,
                    h0_ref, h1_ref, h2_ref, h3_ref, w_ref, gains_ref, gain_two_ref, back_ref, keep_ref, send_ref, h_ref, grads, small):
    rows = lax.broadcasted_iota(jnp.int32, (256, 256), 0)
    taps = taps_ref[...]
    tap_grads = [jnp.zeros((1, 256), F32) for _ in range(3)]
    gain_one = jnp.zeros((1, 1024), F32)
    for i, block in enumerate((h0_ref, h1_ref, h2_ref, h3_ref)):
        h_ref[256 * i : 256 * (i + 1), :] = block[...]
    for s in range(4):
        grad_mixer = gm_ref[s]
        b_part, c_part, x_part = (mixed_ref[s, :, 256 * i : 256 * (i + 1)] for i in range(3))
        grad_cv = grad_mixer * c_part
        lag_one, lag_two = grad_cv * one_ref[s], grad_cv * two_ref[s]
        later = later_ref[s]
        ahead_one = jnp.where(rows == 255, later[0:1], pltpu.roll(lag_one, 255, 0))
        ahead_two = jnp.where(rows == 255, later[2:3], jnp.where(rows == 254, later[1:2], pltpu.roll(lag_two, 254, 0)))
        current = bx_ref[s].astype(F32)
        before = arrived_ref[s].astype(F32)
        back_one = jnp.where(rows == 0, before[1:2], pltpu.roll(current, 1, 0))
        back_two = jnp.where(rows == 0, before[0:1], jnp.where(rows == 1, before[1:2], pltpu.roll(current, 2, 0)))
        for i, term in enumerate((lag_two * back_two, lag_one * back_one, grad_cv * current)):
            tap_grads[i] += jnp.sum(term, axis=0, keepdims=True)
        grad_bx = taps[2:3] * grad_cv + taps[1:2] * ahead_one + taps[0:1] * ahead_two
        grad_bx = grad_bx.astype(BF16).astype(F32)
        at = slice(256 * s, 256 * (s + 1))
        grads[at, 0:256] = (grad_bx * x_part).astype(BF16)
        grads[at, 256:512] = (grad_mixer * cv_ref[s]).astype(BF16)
        grads[at, 512:768] = (grad_bx * b_part).astype(BF16)
        grad_h = dot(grads[at, :], w_ref[...], ((1,), (1,)))
        gain_one += jnp.sum(grad_h * h_ref[at, :].astype(F32), axis=0, keepdims=True)
        if s % 2 == 0:
            keep_ref[s // 2] = grad_h
        else:
            send_ref[s // 2] = grad_h.astype(BF16)
    gain_one = gain_one / gains_ref[0:1, :]
    small[...] = jnp.zeros_like(small)
    for i in range(4):
        small[i : i + 1] = gain_one[:, 256 * i : 256 * (i + 1)]
        small[4 + i : 5 + i] = gain_two_ref[:, 256 * i : 256 * (i + 1)]
    for i in range(3):
        small[8 + i : 9 + i] = tap_grads[i]
    back_ref[:, 128:144, :] = jnp.broadcast_to(small[...].astype(BF16)[None], (32, 16, 256))
    for i in range(3):
        grad_in = dot(h_ref[...], grads[:, 256 * i : 256 * (i + 1)], ((0,), (0,)))
        back_ref[:, 32 * i : 32 * (i + 1), :] = grad_in.astype(BF16).reshape(32, 32, 256)
    for i in range(4):
        back_ref[8 * i : 8 * (i + 1), 96:128, :] = gmix_ref[:, 256 * i : 256 * (i + 1)].reshape(8, 32, 256)


def mix_back(*args):
    vmem = pl.BlockSpec(memory_space=pltpu.VMEM)
    half = (2, 256, 1024)
    return pl.pallas_call(
        mix_back_kernel,
        in_specs=[vmem] * len(args),
        out_specs=[vmem] * 3,
        out_shape=[jax.ShapeDtypeStruct((32, 144, 256), BF16), jax.ShapeDtypeStruct(half, F32), jax.ShapeDtypeStruct(half, BF16)],
        scratch_shapes=[pltpu.VMEM((1024, 1024), BF16), pltpu.VMEM((1024, 768), BF16), pltpu.VMEM((16, 256), F32)],
        compiler_params=pltpu.CompilerParams(vmem_limit_bytes=40 * 1024 * 1024),
        cost_estimate=pl.CostEstimate(flops=4 * 10**9, bytes_accessed=10**7, transcendentals=0),
    )(*args)


def pack_columns_kernel(gate_ref, up_ref, out_ref):
    for j in range(3):
        at = 384 * j
        out_ref[96 * j : 96 * j + 32, :] = gate_ref[:, at : at + 256]
        out_ref[96 * j + 32 : 96 * j + 64, 0:128] = gate_ref[:, at + 256 : at + 384]
        out_ref[96 * j + 32 : 96 * j + 64, 128:256] = up_ref[:, at : at + 128]
        out_ref[96 * j + 64 : 96 * j + 96, :] = up_ref[:, at + 128 : at + 384]


def pack_columns(w_gate, w_up):
    vmem = pl.BlockSpec(memory_space=pltpu.VMEM)
    return pl.pallas_call(
        pack_columns_kernel,
        in_specs=[vmem] * 2,
        out_specs=vmem,
        out_shape=jax.ShapeDtypeStruct((288, 256), BF16),
        compiler_params=pltpu.CompilerParams(vmem_limit_bytes=4 * 1024 * 1024),
    )(w_gate, w_up)


def local(tokens, token_pos, w_in, w_mix, w_gate, w_up, w_down, conv_weight, norm_gains, cotangent):
    inputs = tokens[0]
    grad_result = cotangent[0]
    rows, model = inputs.shape
    f_index = lax.axis_index(FSDP)

    line = jnp.concatenate([norm_gains[:1], norm_gains[1:], jnp.minimum(token_pos, 2).astype(BF16)], axis=1)
    start = gather_group(jnp.concatenate([w_in, line, jnp.zeros((15, 768), BF16)], axis=0)[None])
    in_blocks = []
    for part in range(3):
        column = 4 * part + f_index
        at = (column // 3 ^ f_index, 0, column % 3 * 256)
        in_blocks.append(lax.dynamic_slice(start, at, (1, 32, 256))[0])
    gain_rows = in_member_order(start[:, 32, :512].astype(F32)).reshape(4, 2, 256).transpose(1, 0, 2).reshape(2, 1024)
    positions = start[:, 32, 512:]
    mask_one = (positions >= 1).astype(F32)[:, :, None]
    mask_two = (positions >= 2).astype(F32)[:, :, None]
    conv_taps = conv_weight.astype(F32)

    row_blocks = lax.ppermute(jnp.concatenate([w_mix, w_down], axis=0), ALL, ROW_ROUTE)
    own = jnp.concatenate([pack_columns(w_gate, w_up), row_blocks[32:], *in_blocks, row_blocks[:32]], axis=0)
    both = in_zh_order(own, swap(own, "zh"))
    first_copies = jnp.broadcast_to(both[:, 432:], (16, 2, 128, 256))
    first_all = lax.all_to_all(first_copies, YX, 0, 0, tiled=True)
    second_all = lax.all_gather(both[:, :432].reshape(864, 256), YX, axis=0, tiled=True).reshape(16, 2, 432, 256)
    grad_low_all = group_blocks(grad_result.astype(BF16))
    first_all = after(first_all, *grad_low_all)
    in_rows = first_all.transpose(1, 0, 2, 3)
    w_in_f = jnp.concatenate([in_rows[:, :, 32 * i : 32 * (i + 1)].reshape(1024, 256) for i in range(3)], axis=1)
    w_mix_f = jnp.concatenate(
        [in_rows[i // 2, i % 2 * 8 : i % 2 * 8 + 8, 96:].reshape(256, 256) for i in range(4)], axis=1
    )

    normed1, inv_one, hidden1 = norm_forward(inputs, gain_rows[0])
    hidden1_blocks = group_blocks(hidden1)
    hidden1_all = jnp.concatenate(hidden1_blocks, axis=0)

    mixed = dot(hidden1_all, w_in_f, ((1,), (0,))).reshape(4, rows, 768)
    b_part, c_part, x_part = mixed[..., :256], mixed[..., 256:512], mixed[..., 512:]
    product_bx = (b_part * x_part).astype(BF16)
    arrived = lax.ppermute(product_bx[:, -2:], SEQ, [(i, i + 1) for i in range(31)])
    extended = jnp.concatenate([arrived, product_bx], axis=1).astype(F32)
    current, back_one, back_two = extended[:, 2:], extended[:, 1:-1], extended[:, :-2]
    conv_val = conv_taps[2] * current + conv_taps[1] * mask_one * back_one + conv_taps[0] * mask_two * back_two
    mixer = (c_part * conv_val).astype(BF16).reshape(4 * rows, 256)
    branch = scatter_group(dot(mixer, w_mix_f, ((1,), (0,))).reshape(4, rows, model))
    middle = inputs + branch
    normed2, inv_two, hidden2 = norm_forward(middle, gain_rows[1])
    hidden2_all = group_blocks(hidden2)

    out_keep, out_send, grad_keep, grad_send, back_pack = ffn(hidden2_all, grad_low_all, second_all)
    ffn_sums = lax.psum_scatter(back_pack.reshape(16 * 864, 256), YX, scatter_dimension=0, tiled=True).reshape(2, 432, 256)
    ordered = in_zh_order(ffn_sums[0], ffn_sums[1])
    ffn_own = ordered[0].astype(F32) + swap(ordered[1], "zh").astype(F32)
    grad_down = lax.ppermute(ffn_own[288:].astype(BF16), ALL, ROW_BACK).astype(F32)

    grad_hidden2 = finish_scatter(grad_keep, grad_send)
    grad_norm_two, gain_two = norm_backward(grad_hidden2, normed2, inv_two, gain_rows[1])
    grad_middle = grad_result + grad_norm_two
    grad_branch_blocks = group_blocks(grad_middle.astype(BF16))
    grad_branch_all = jnp.concatenate(grad_branch_blocks, axis=0)
    out_got = swap(out_send, "c").astype(F32)
    out_far = after((out_keep[1] + out_got[1]).astype(BF16), grad_branch_blocks[1])
    out_far = swap(out_far, "zl")
    result = middle + out_keep[0] + out_got[0] + out_far.astype(F32)
    grad_mix = dot(mixer, grad_branch_all, ((0,), (0,))).astype(BF16)
    grad_mixer = dot(grad_branch_all, w_mix_f, ((1,), (1,))).reshape(4, rows, 256)
    edge = grad_mixer[:, :2] * c_part[:, :2]
    later = jnp.concatenate([edge[:, :1] * mask_one[:, :1], edge * mask_two[:, :2]], axis=1)
    later = lax.ppermute(later, SEQ, [(i + 1, i) for i in range(31)])
    first_back, keep, send = mix_back(
        after(grad_mixer, out_far),
        grad_mix,
        mixed,
        conv_val,
        product_bx,
        arrived,
        later,
        mask_one,
        mask_two,
        conv_taps,
        *hidden1_blocks,
        w_in_f,
        gain_rows,
        gain_two[None],
    )
    first_got = lax.all_to_all(first_back, SEQ, 0, 0, tiled=True).reshape(32, 144, 256)
    first_got, _ = lax.optimization_barrier((first_got, grad_down))
    first_sums = jnp.sum(first_got.astype(F32), axis=0)
    conv_total = first_sums[136:139]
    group_sums = gather_group(first_sums[None].astype(BF16))
    in_own = []
    for i in range(3):
        column = 3 * f_index + i
        in_own.append(lax.dynamic_slice(group_sums, (column % 4 ^ f_index, column // 4 * 32, 0), (1, 32, 256))[0])
    grad_in_own = jnp.concatenate(in_own, axis=1).astype(F32)
    gain_terms = group_sums[:, 128:136].reshape(4, 2, 4, 256).astype(F32)
    gains_total = jnp.sum(lax.dynamic_index_in_dim(gain_terms, f_index, axis=2, keepdims=False), axis=0)
    grad_mix_own = lax.ppermute(first_sums[96:128].astype(BF16), ALL, ROW_BACK).astype(F32)

    grad_hidden1 = finish_scatter(keep, send)
    grad_norm_one, _ = norm_backward(grad_hidden1, normed1, inv_one, gain_rows[0])
    grad_inputs = grad_middle + grad_norm_one

    grad_gu = ffn_own[:288].reshape(9, 32, 256)
    grad_gate = [c for i in (0, 3, 6) for c in (grad_gu[i], grad_gu[i + 1, :, :128])]
    grad_up = [c for i in (0, 3, 6) for c in (grad_gu[i + 1, :, 128:], grad_gu[i + 2])]
    return (
        result[None],
        grad_inputs[None],
        grad_in_own,
        grad_mix_own,
        jnp.concatenate(grad_gate, axis=1),
        jnp.concatenate(grad_up, axis=1),
        grad_down,
        conv_total,
        gains_total,
    )


def solution(mesh):
    fine = Mesh(mesh.devices.reshape(2, 4, 4, 2, 2), ALL)
    tokens, weight, small = P(FSDP, SEQ, None), P(SEQ, FSDP), P(None, FSDP)
    return jax.shard_map(
        local,
        mesh=fine,
        in_specs=(tokens, P(FSDP, SEQ), weight, weight, weight, weight, weight, small, small, tokens),
        out_specs=(tokens, tokens, weight, weight, weight, weight, weight, small, small),
        check_vma=False,
    )
```

```python
import functools

import jax
import jax.numpy as jnp
from jax import lax
from jax.experimental import pallas as pl
from jax.experimental.pallas import tpu as pltpu
from jax.sharding import Mesh
from jax.sharding import PartitionSpec as P

EPSILON = 1e-05
SEQ = ("zh", "y", "x")
YX = ("y", "x")
FSDP = ("zl", "c")
ALL = SEQ + FSDP
BF16 = jnp.bfloat16
F32 = jnp.float32


def swap(x, axis):
    return lax.ppermute(x, axis, [(0, 1), (1, 0)])


def group_blocks(x):
    far = swap(x, "zl")
    near = swap(x, "c")
    return (x, near, far, swap(far, "c"))


def gather_group(x):
    across = lax.ppermute(x, FSDP, [(f, 3 - f) for f in range(4)])
    return jnp.concatenate((x, swap(x, "c"), swap(x, "zl"), across), axis=0)


def after(x, *others):
    return lax.optimization_barrier((x, *others))[0]


def scatter_group(partial):
    return finish_scatter(partial[0::2], partial[1::2].astype(BF16))


def finish_scatter(keep, send):
    got = swap(send, "c")
    far = swap((keep[1] + got[1].astype(F32)).astype(BF16), "zl")
    return keep[0] + got[0].astype(F32) + far.astype(F32)


def norm_forward(values, norm_gain):
    inv_rms = lax.rsqrt(jnp.mean(values * values, axis=-1, keepdims=True) + EPSILON)
    normed = values * inv_rms
    return (normed, inv_rms, (normed * norm_gain).astype(BF16))


def norm_backward(grad_hidden, normed, inv_rms, norm_gain):
    grad_normed = grad_hidden * norm_gain
    inner_mean = jnp.mean(grad_normed * normed, axis=-1, keepdims=True)
    return (inv_rms * (grad_normed - normed * inner_mean), jnp.sum(grad_hidden * normed, axis=0))


def dot(a, b, dims):
    return lax.dot_general(a, b, (dims, ((), ())), preferred_element_type=F32)


ROW_ROUTE = [(s * 4 + f, (f * 8 + s % 8) * 4 + s // 8) for s in range(32) for f in range(4)]
ROW_BACK = [(b, a) for a, b in ROW_ROUTE]


def in_zh_order(mine, other):
    first = lax.axis_index("zh") == 0
    return jnp.where(first, jnp.stack([mine, other]), jnp.stack([other, mine]))


def in_member_order(x):
    x = jnp.where(lax.axis_index("c") == 1, jnp.stack([x[1], x[0], x[3], x[2]]), x)
    return jnp.where(lax.axis_index("zl") == 1, jnp.stack([x[2], x[3], x[0], x[1]]), x)


def ffn_kernel(rows_t, *refs):
    h_blocks, gl_blocks = refs[:4], refs[4:8]
    wg_ref, wd_ref, out_keep, out_send, gh_keep, gh_send, packed = refs[8:15]
    h_ref, gl_ref, wj, wdj, act_s, gp_s, out_acc, gh_acc, g_s, d_s, sems = refs[15:]
    j = pl.program_id(0)
    for k in range(3):
        for zh in range(2):
            wj[512 * zh : 512 * (zh + 1), 256 * k : 256 * (k + 1)] = wg_ref[:, zh, 32 * k : 32 * (k + 1), :].reshape(512, 256)
    for i in range(8):
        at = 8 * j + i
        for f in range(4):
            wdj[48 * i : 48 * (i + 1), 256 * f : 256 * (f + 1)] = wd_ref[
                f % 2 * 8 + at // 3, f // 2, pl.ds(pl.multiple_of(at % 3 * 48, 16), 48), :
            ]

    @pl.when(j == 0)
    def _():
        for i in range(4):
            h_ref[256 * i : 256 * (i + 1), :] = h_blocks[i][...]
            gl_ref[256 * i : 256 * (i + 1), :] = gl_blocks[i][...]
        out_acc[...] = jnp.zeros_like(out_acc)
        gh_acc[...] = jnp.zeros_like(gh_acc)

    def step(t, _):
        rows = pl.ds(pl.multiple_of(t * rows_t, rows_t), rows_t)
        gu = dot(h_ref[rows, :], wj[...], ((1,), (0,)))
        gate, up = gu[:, :384], gu[:, 384:]
        sig = jax.nn.sigmoid(gate)
        silu = gate * sig
        act = (silu * up).astype(BF16)
        grad_act = dot(gl_ref[rows, :], wdj[...], ((1,), (1,)))
        d_gate = grad_act * up * (sig * (1.0 + gate * (1.0 - sig)))
        d_up = grad_act * silu
        act_s[rows, :] = act
        gp_s[rows, :384] = d_gate.astype(BF16)
        gp_s[rows, 384:] = d_up.astype(BF16)
        out_acc[rows, :] += dot(act, wdj[...], ((1,), (0,)))
        gh_acc[rows, :] += dot(gp_s[rows, :], wj[...], ((1,), (1,)))
        return 0

    lax.fori_loop(0, 1024 // rows_t, step, 0)
    for k in range(3):
        acc = dot(h_ref[...], gp_s[:, 256 * k : 256 * (k + 1)], ((0,), (0,))).astype(BF16)
        for zh in range(2):
            g_s[j, :, zh, 32 * k : 32 * (k + 1), :] = acc[512 * zh : 512 * (zh + 1)].reshape(16, 32, 256)
    for f in range(4):
        acc = dot(act_s[...], gl_ref[:, 256 * f : 256 * (f + 1)], ((0,), (0,))).astype(BF16)
        for i in range(8):
            at = 8 * j + i
            d_s[f % 2 * 8 + at // 3, f // 2, pl.ds(pl.multiple_of(at % 3 * 48, 16), 48), :] = acc[48 * i : 48 * (i + 1)]

    def send(i):
        return pltpu.make_async_copy(g_s.at[i], packed.at[:, :, pl.ds(96 * i, 96), :], sems.at[i])

    for i in range(3):
        @pl.when(j == i)
        def _():
            send(i).start()

    @pl.when(j == 2)
    def _():
        last = pltpu.make_async_copy(d_s, packed.at[:, :, pl.ds(288, 144), :], sems.at[3])
        last.start()
        for i in range(2):
            out_keep[i] = out_acc[512 * i : 512 * i + 256]
            gh_keep[i] = gh_acc[512 * i : 512 * i + 256]
            out_send[i] = out_acc[512 * i + 256 : 512 * (i + 1)].astype(BF16)
            gh_send[i] = gh_acc[512 * i + 256 : 512 * (i + 1)].astype(BF16)
        for i in range(3):
            send(i).wait()
        last.wait()

def ffn(h, gl, pack, rows_t=512):
    whole = lambda shape: pl.BlockSpec(shape, lambda j: (0,) * len(shape))
    once = lambda shape: pl.BlockSpec(shape, lambda j: (0,) * len(shape), pipeline_mode=pl.Buffered(1))
    half = (2, 256, 1024)
    return pl.pallas_call(
        functools.partial(ffn_kernel, rows_t),
        grid=(3,),
        in_specs=[once((256, 1024))] * 8 + [pl.BlockSpec((16, 2, 96, 256), lambda j: (0, 0, j, 0)),
                  pl.BlockSpec((16, 2, 144, 256), lambda j: (0, 0, 2, 0), pipeline_mode=pl.Buffered(1))],
        out_specs=[once(half)] * 4 + [pl.BlockSpec(memory_space=pl.ANY)],
        out_shape=[jax.ShapeDtypeStruct(half, F32), jax.ShapeDtypeStruct(half, BF16)] * 2 + [jax.ShapeDtypeStruct((16, 2, 432, 256), BF16)],
        scratch_shapes=[pltpu.VMEM((1024, 1024), BF16)] * 2 + [pltpu.VMEM((1024, 768), BF16), pltpu.VMEM((384, 1024), BF16), pltpu.VMEM((1024, 384), BF16), pltpu.VMEM((1024, 768), BF16),
            pltpu.VMEM((1024, 1024), F32), pltpu.VMEM((1024, 1024), F32), pltpu.VMEM((3, 16, 2, 96, 256), BF16), pltpu.VMEM((16, 2, 144, 256), BF16),
            pltpu.SemaphoreType.DMA((4,))],
        compiler_params=pltpu.CompilerParams(vmem_limit_bytes=56 * 1024 * 1024, dimension_semantics=("arbitrary",)),
        cost_estimate=pl.CostEstimate(flops=22 * 10**9, bytes_accessed=30 * 10**6, transcendentals=2 * 10**6),
    )(*h, *gl, pack, pack)


def mix_back_kernel(gm_ref, gmix_ref, mixed_ref, cv_ref, bx_ref, arrived_ref, later_ref, one_ref, two_ref, taps_ref,
                    h0_ref, h1_ref, h2_ref, h3_ref, w_ref, gains_ref, gain_two_ref, back_ref, keep_ref, send_ref, h_ref, grads, small):
    rows = lax.broadcasted_iota(jnp.int32, (256, 256), 0)
    taps = taps_ref[...]
    tap_grads = [jnp.zeros((1, 256), F32) for _ in range(3)]
    gain_one = jnp.zeros((1, 1024), F32)
    for i, block in enumerate((h0_ref, h1_ref, h2_ref, h3_ref)):
        h_ref[256 * i : 256 * (i + 1), :] = block[...]
    for s in range(4):
        grad_mixer = gm_ref[s]
        b_part, c_part, x_part = (mixed_ref[s, :, 256 * i : 256 * (i + 1)] for i in range(3))
        grad_cv = grad_mixer * c_part
        lag_one, lag_two = grad_cv * one_ref[s], grad_cv * two_ref[s]
        later = later_ref[s]
        ahead_one = jnp.where(rows == 255, later[0:1], pltpu.roll(lag_one, 255, 0))
        ahead_two = jnp.where(rows == 255, later[2:3], jnp.where(rows == 254, later[1:2], pltpu.roll(lag_two, 254, 0)))
        current = bx_ref[s].astype(F32)
        before = arrived_ref[s].astype(F32)
        back_one = jnp.where(rows == 0, before[1:2], pltpu.roll(current, 1, 0))
        back_two = jnp.where(rows == 0, before[0:1], jnp.where(rows == 1, before[1:2], pltpu.roll(current, 2, 0)))
        for i, term in enumerate((lag_two * back_two, lag_one * back_one, grad_cv * current)):
            tap_grads[i] += jnp.sum(term, axis=0, keepdims=True)
        grad_bx = taps[2:3] * grad_cv + taps[1:2] * ahead_one + taps[0:1] * ahead_two
        grad_bx = grad_bx.astype(BF16).astype(F32)
        at = slice(256 * s, 256 * (s + 1))
        grads[at, 0:256] = (grad_bx * x_part).astype(BF16)
        grads[at, 256:512] = (grad_mixer * cv_ref[s]).astype(BF16)
        grads[at, 512:768] = (grad_bx * b_part).astype(BF16)
        grad_h = dot(grads[at, :], w_ref[...], ((1,), (1,)))
        gain_one += jnp.sum(grad_h * h_ref[at, :].astype(F32), axis=0, keepdims=True)
        if s % 2 == 0:
            keep_ref[s // 2] = grad_h
        else:
            send_ref[s // 2] = grad_h.astype(BF16)
    gain_one = gain_one / gains_ref[0:1, :]
    small[...] = jnp.zeros_like(small)
    for i in range(4):
        small[i : i + 1] = gain_one[:, 256 * i : 256 * (i + 1)]
        small[4 + i : 5 + i] = gain_two_ref[:, 256 * i : 256 * (i + 1)]
    for i in range(3):
        small[8 + i : 9 + i] = tap_grads[i]
    back_ref[:, 128:144, :] = jnp.broadcast_to(small[...].astype(BF16)[None], (32, 16, 256))
    for i in range(3):
        grad_in = dot(h_ref[...], grads[:, 256 * i : 256 * (i + 1)], ((0,), (0,)))
        back_ref[:, 32 * i : 32 * (i + 1), :] = grad_in.astype(BF16).reshape(32, 32, 256)
    for i in range(4):
        back_ref[8 * i : 8 * (i + 1), 96:128, :] = gmix_ref[:, 256 * i : 256 * (i + 1)].reshape(8, 32, 256)


def mix_back(*args):
    vmem = pl.BlockSpec(memory_space=pltpu.VMEM)
    half = (2, 256, 1024)
    return pl.pallas_call(
        mix_back_kernel,
        in_specs=[vmem] * len(args),
        out_specs=[vmem] * 3,
        out_shape=[jax.ShapeDtypeStruct((32, 144, 256), BF16), jax.ShapeDtypeStruct(half, F32), jax.ShapeDtypeStruct(half, BF16)],
        scratch_shapes=[pltpu.VMEM((1024, 1024), BF16), pltpu.VMEM((1024, 768), BF16), pltpu.VMEM((16, 256), F32)],
        compiler_params=pltpu.CompilerParams(vmem_limit_bytes=40 * 1024 * 1024),
        cost_estimate=pl.CostEstimate(flops=4 * 10**9, bytes_accessed=10**7, transcendentals=0),
    )(*args)


def pack_columns_kernel(gate_ref, up_ref, out_ref):
    for j in range(3):
        at = 384 * j
        out_ref[96 * j : 96 * j + 32, :] = gate_ref[:, at : at + 256]
        out_ref[96 * j + 32 : 96 * j + 64, 0:128] = gate_ref[:, at + 256 : at + 384]
        out_ref[96 * j + 32 : 96 * j + 64, 128:256] = up_ref[:, at : at + 128]
        out_ref[96 * j + 64 : 96 * j + 96, :] = up_ref[:, at + 128 : at + 384]


def pack_columns(w_gate, w_up):
    vmem = pl.BlockSpec(memory_space=pltpu.VMEM)
    return pl.pallas_call(
        pack_columns_kernel,
        in_specs=[vmem] * 2,
        out_specs=vmem,
        out_shape=jax.ShapeDtypeStruct((288, 256), BF16),
        compiler_params=pltpu.CompilerParams(vmem_limit_bytes=4 * 1024 * 1024),
    )(w_gate, w_up)


def local(tokens, token_pos, w_in, w_mix, w_gate, w_up, w_down, conv_weight, norm_gains, cotangent):
    inputs = tokens[0]
    grad_result = cotangent[0]
    rows, model = inputs.shape
    f_index = lax.axis_index(FSDP)

    line = jnp.concatenate([norm_gains[:1], norm_gains[1:], jnp.minimum(token_pos, 2).astype(BF16)], axis=1)
    start = gather_group(jnp.concatenate([w_in, line, jnp.zeros((15, 768), BF16)], axis=0)[None])
    in_blocks = []
    for part in range(3):
        column = 4 * part + f_index
        at = (column // 3 ^ f_index, 0, column % 3 * 256)
        in_blocks.append(lax.dynamic_slice(start, at, (1, 32, 256))[0])
    gain_rows = in_member_order(start[:, 32, :512].astype(F32)).reshape(4, 2, 256).transpose(1, 0, 2).reshape(2, 1024)
    positions = start[:, 32, 512:]
    mask_one = (positions >= 1).astype(F32)[:, :, None]
    mask_two = (positions >= 2).astype(F32)[:, :, None]
    conv_taps = conv_weight.astype(F32)

    row_blocks = lax.ppermute(jnp.concatenate([w_mix, w_down], axis=0), ALL, ROW_ROUTE)
    own = jnp.concatenate([pack_columns(w_gate, w_up), row_blocks[32:], *in_blocks, row_blocks[:32]], axis=0)
    both = in_zh_order(own, swap(own, "zh"))
    first_copies = jnp.broadcast_to(both[:, 432:], (16, 2, 128, 256))
    first_all = lax.all_to_all(first_copies, YX, 0, 0, tiled=True)
    second_all = lax.all_gather(both[:, :432].reshape(864, 256), YX, axis=0, tiled=True).reshape(16, 2, 432, 256)
    grad_low_all = group_blocks(grad_result.astype(BF16))
    first_all = after(first_all, *grad_low_all)
    in_rows = first_all.transpose(1, 0, 2, 3)
    w_in_f = jnp.concatenate([in_rows[:, :, 32 * i : 32 * (i + 1)].reshape(1024, 256) for i in range(3)], axis=1)
    w_mix_f = jnp.concatenate(
        [in_rows[i // 2, i % 2 * 8 : i % 2 * 8 + 8, 96:].reshape(256, 256) for i in range(4)], axis=1
    )

    normed1, inv_one, hidden1 = norm_forward(inputs, gain_rows[0])
    hidden1_blocks = group_blocks(hidden1)
    hidden1_all = jnp.concatenate(hidden1_blocks, axis=0)

    mixed = dot(hidden1_all, w_in_f, ((1,), (0,))).reshape(4, rows, 768)
    b_part, c_part, x_part = mixed[..., :256], mixed[..., 256:512], mixed[..., 512:]
    product_bx = (b_part * x_part).astype(BF16)
    arrived = lax.ppermute(product_bx[:, -2:], SEQ, [(i, i + 1) for i in range(31)])
    extended = jnp.concatenate([arrived, product_bx], axis=1).astype(F32)
    current, back_one, back_two = extended[:, 2:], extended[:, 1:-1], extended[:, :-2]
    conv_val = conv_taps[2] * current + conv_taps[1] * mask_one * back_one + conv_taps[0] * mask_two * back_two
    mixer = (c_part * conv_val).astype(BF16).reshape(4 * rows, 256)
    branch = scatter_group(dot(mixer, w_mix_f, ((1,), (0,))).reshape(4, rows, model))
    middle = inputs + branch
    normed2, inv_two, hidden2 = norm_forward(middle, gain_rows[1])
    hidden2_all = group_blocks(hidden2)

    out_keep, out_send, grad_keep, grad_send, back_pack = ffn(hidden2_all, grad_low_all, second_all)
    ffn_sums = lax.psum_scatter(back_pack.reshape(16 * 864, 256), YX, scatter_dimension=0, tiled=True).reshape(2, 432, 256)
    ordered = in_zh_order(ffn_sums[0], ffn_sums[1])
    ffn_own = ordered[0].astype(F32) + swap(ordered[1], "zh").astype(F32)
    grad_down = lax.ppermute(ffn_own[288:].astype(BF16), ALL, ROW_BACK).astype(F32)

    grad_hidden2 = finish_scatter(grad_keep, grad_send)
    grad_norm_two, gain_two = norm_backward(grad_hidden2, normed2, inv_two, gain_rows[1])
    grad_middle = grad_result + grad_norm_two
    grad_branch_blocks = group_blocks(grad_middle.astype(BF16))
    grad_branch_all = jnp.concatenate(grad_branch_blocks, axis=0)
    out_got = swap(out_send, "c")
    out_far = after((out_keep[1] + out_got[1].astype(F32)).astype(BF16), grad_branch_blocks[1])
    out_far = swap(out_far, "zl")
    grad_mix = dot(mixer, grad_branch_all, ((0,), (0,))).astype(BF16)
    grad_mixer = dot(grad_branch_all, w_mix_f, ((1,), (1,))).reshape(4, rows, 256)
    edge = grad_mixer[:, :2] * c_part[:, :2]
    later = jnp.concatenate([edge[:, :1] * mask_one[:, :1], edge * mask_two[:, :2]], axis=1)
    later = lax.ppermute(later, SEQ, [(i + 1, i) for i in range(31)])
    first_back, keep, send = mix_back(
        after(grad_mixer, out_far),
        grad_mix,
        mixed,
        conv_val,
        product_bx,
        arrived,
        later,
        mask_one,
        mask_two,
        conv_taps,
        *hidden1_blocks,
        w_in_f,
        gain_rows,
        gain_two[None],
    )
    first_got = lax.all_to_all(first_back, SEQ, 0, 0, tiled=True).reshape(32, 144, 256)
    first_got, _ = lax.optimization_barrier((first_got, grad_down))
    first_sums = jnp.sum(first_got.astype(F32), axis=0)
    result = middle + out_keep[0] + out_got[0].astype(F32) + after(out_far, first_sums).astype(F32)
    conv_total = first_sums[136:139]
    group_sums = gather_group(first_sums[None].astype(BF16))
    in_own = []
    for i in range(3):
        column = 3 * f_index + i
        in_own.append(lax.dynamic_slice(group_sums, (column % 4 ^ f_index, column // 4 * 32, 0), (1, 32, 256))[0])
    grad_in_own = jnp.concatenate(in_own, axis=1).astype(F32)
    gain_terms = group_sums[:, 128:136].reshape(4, 2, 4, 256).astype(F32)
    gains_total = jnp.sum(lax.dynamic_index_in_dim(gain_terms, f_index, axis=2, keepdims=False), axis=0)
    grad_mix_own = lax.ppermute(first_sums[96:128].astype(BF16), ALL, ROW_BACK).astype(F32)

    grad_hidden1 = finish_scatter(keep, send)
    grad_norm_one, _ = norm_backward(grad_hidden1, normed1, inv_one, gain_rows[0])
    grad_inputs = grad_middle + grad_norm_one

    grad_gu = ffn_own[:288].reshape(9, 32, 256)
    grad_gate = [c for i in (0, 3, 6) for c in (grad_gu[i], grad_gu[i + 1, :, :128])]
    grad_up = [c for i in (0, 3, 6) for c in (grad_gu[i + 1, :, 128:], grad_gu[i + 2])]
    return (
        result[None],
        grad_inputs[None],
        grad_in_own,
        grad_mix_own,
        jnp.concatenate(grad_gate, axis=1),
        jnp.concatenate(grad_up, axis=1),
        grad_down,
        conv_total,
        gains_total,
    )


def solution(mesh):
    fine = Mesh(mesh.devices.reshape(2, 4, 4, 2, 2), ALL)
    tokens, weight, small = P(FSDP, SEQ, None), P(SEQ, FSDP), P(None, FSDP)
    return jax.shard_map(
        local,
        mesh=fine,
        in_specs=(tokens, P(FSDP, SEQ), weight, weight, weight, weight, weight, small, small, tokens),
        out_specs=(tokens, tokens, weight, weight, weight, weight, weight, small, small),
        check_vma=False,
    )
```
